1024 devices in a mesh: rows: 64 (over y, z), feat: 16 (over x, core).
Axes of the slice: x: 8, y: 8, z: 8, core: 2. Of those that a mesh axis runs over, the one named last changes fastest.
Arguments:
- features: bfloat16 [262144, 768], P('rows', 'feat'), may hold values from -6 to 6
- w1_self: bfloat16 [768, 1024], replicated, may hold values from -0.21875 to 0.21875
- w1_neigh: bfloat16 [768, 1024], replicated, may hold values from -0.21875 to 0.21875
- bias_one: float32 [1024], replicated, may hold values from -3 to 3
- w2_self: bfloat16 [1024, 1024], replicated, may hold values from -0.1875 to 0.1875
- w2_neigh: bfloat16 [1024, 1024], replicated, may hold values from -0.1875 to 0.1875
- bias_two: float32 [1024], replicated, may hold values from -3 to 3
- owner: int32 [262144, 1], P('rows'), may hold values from 0 to 63; in each aligned block of 4096 rows (0 to 4095, 4096 to 8191, ...) at most 80 rows name the same one
- row_index: int32 [262144], P('rows'), may hold values from 0 to 4095
- count_one: int32 [16384], P('rows'), may hold values from 1 to 15
- neighbours_two: int32 [16384, 10], P(('rows', 'feat')), may hold values from 0 to 15
- count_two: int32 [16384], P(('rows', 'feat')), may hold values from 1 to 10
Outputs:
- embedding: bfloat16 [16384, 1024], P(('rows', 'feat'))
The draws below stay inside these ranges and needn't reach their ends.
Inputs may be any that keep to these rules, and one draw needn't show every extreme that they name: Among the 4096 rows of one index of rows (aligned blocks of owner), no owner is named more than 80 times, a bound that some block reaches. `neighbours_two`: indices within the target's own block of 16 targets.
All inputs are finite; a program needn't handle non-finite values.
Results may differ from the reference program's by a relative error of at most 0.0051.
Values may be sent and summed in bfloat16 or wider, within the bound.
No kernel may reach another device: no remote copies, remote signals or barrier semaphores. Data moves between devices by JAX's collectives and lax.ppermute only.
A program may use at most 32 MiB of HBM per device.

```python
import math
import jax
import jax.numpy as jnp
import numpy as np
from jax import lax

F = 768
HID = 1024
K1 = 15
K2 = 10
TGT_DEV = 16
NODE_DEV = 4096
REQ = 4096
CAP = 80
NODES = 262144
REQS = 262144
TARGETS = 16384
N_ROWS = 64
N_FEAT = 16
DEVICES = 1024


def set_ends(entries, own_key, least, largest):
    longest = entries.shape.index(max(entries.shape))
    spots = []
    for shift in (0, 1):
        where = [jax.random.randint(jax.random.fold_in(own_key, axis), (), 0, length) for axis, length in enumerate(entries.shape)]
        where[longest] = (where[longest] + shift) % entries.shape[longest]
        spots.append(tuple(where))
    return entries.at[spots[0]].set(least).at[spots[1]].set(largest)


def steps_of(own_key, shape, pieces, low, largest):
    factor_of = 1.0
    for axis_at, shards_of in pieces:
        heights = jax.random.uniform(jax.random.fold_in(jax.random.fold_in(own_key, 6), axis_at), (shards_of,), jnp.float32, low / len(pieces), largest / len(pieces))
        factor_of = factor_of * jnp.repeat(jnp.exp(heights), shape[axis_at] // shards_of).reshape((-1,) + (1,) * (len(shape) - 1 - axis_at))
    return factor_of


def routed_block(rng, own, number, rows, number_of, top, most, slope):
    sequence = jax.random.permutation(rng, number_of)
    crowded, usual = shares(number_of, rows * top, most, slope, True), shares(number_of, rows * top, most, slope, False)
    places = jnp.arange(number_of)

    def named(sizes, turn):
        used = int((sizes > 0).sum())
        fixed = max(1, used // 4)
        moved = fixed + (places - fixed + turn * (used - fixed)) % max(1, number_of - fixed)
        return jnp.zeros((number_of,), jnp.int32).at[sequence[jnp.where(places < fixed, places, moved)]].set(jnp.asarray(sizes, jnp.int32))

    sizes = jnp.where(number % 4 == 0, named(crowded, number // 4), named(usual, number - number // 4 - 1))
    mixed = jax.random.permutation(jax.random.fold_in(own, 3), number_of)
    donor, sink = mixed[0:number_of // 2 * 2:2], mixed[1:number_of // 2 * 2:2]
    slack = jnp.minimum(sizes[donor] - 1, most - sizes[sink]) // 2
    slack = jnp.where((donor == sequence[0]) | (sink == sequence[0]) | (sizes[sink] == 0), 0, jnp.maximum(slack, 0))
    moved = jax.random.randint(jax.random.fold_in(own, 4), (number_of // 2,), 0, 1 << 20) % (slack + 1)
    sizes = sizes.at[donor].add(-moved).at[sink].add(moved)
    labels = jnp.searchsorted(jnp.cumsum(sizes), jnp.arange(rows * top), side="right").astype(jnp.int32)
    grid = labels.reshape(top, rows).T
    grid = grid[jax.random.permutation(jax.random.fold_in(own, 1), rows)]
    turn = jax.random.randint(jax.random.fold_in(own, 2), (rows, 1), 0, top)
    return jnp.take_along_axis(grid, (jnp.arange(top)[None, :] + turn) % top, axis=1)


def shares(number_of, total, reach, skew, full):
    loads = [(1 << 20) // math.isqrt(grade ** skew) + 1 for grade in range(1, number_of + 1)]
    largest = reach if full else min(reach, max(-(-total // number_of), total * loads[0] // sum(loads)))
    least = 1 if total - largest >= number_of - 1 else 0
    holding, surplus = [largest] + [least] * (number_of - 1), total - largest - least * (number_of - 1)
    while surplus > 0:
        candidates = [i for i in range(1, number_of) if holding[i] < largest] or [i for i in range(1, number_of) if holding[i] < reach]
        mass, budget = sum([loads[i] for i in candidates]), surplus
        for i in candidates:
            more = min(reach - holding[i], max(1, budget * loads[i] // mass), surplus)
            holding[i] = holding[i] + more
            surplus = surplus - more
    return np.array(holding)


def gaussian(own_key, dims, width, reach, shards=(), dtype=jnp.bfloat16):
    level = steps_of(own_key, dims, shards, -0.22, 0.18) if shards else 1.0
    array = jax.random.normal(own_key, dims, jnp.float32) * width * level
    return jnp.minimum(jnp.maximum(array, -reach), reach).astype(dtype)


def setup_inputs(seed: int = 0) -> dict:
    seeds = jax.random.split(jax.random.key(seed), 13)
    features = gaussian(seeds[0], (NODES, F), 1.0, 6.0, ((0, 64), (1, 16)))
    w1_self = gaussian(seeds[1], (F, HID), F ** -0.5, 0.21875)
    w1_neigh = gaussian(seeds[2], (F, HID), F ** -0.5, 0.21875)
    bias_one = gaussian(seeds[3], (HID,), 0.5, 3.0, (), jnp.float32)
    w2_self = gaussian(seeds[4], (HID, HID), HID ** -0.5, 0.1875)
    w2_neigh = gaussian(seeds[5], (HID, HID), HID ** -0.5, 0.1875)
    bias_two = gaussian(seeds[6], (HID,), 0.5, 3.0, (), jnp.float32)
    owner_keys = jax.random.split(jax.random.fold_in(seeds[7], 1), REQS // REQ)
    owner_turns = jax.random.permutation(jax.random.fold_in(seeds[7], 3), REQS // REQ)
    owner = jax.vmap(lambda own, number: routed_block(jax.random.fold_in(seeds[7], 2), own, number, REQ, N_ROWS, 1, CAP, 2))(owner_keys, owner_turns).reshape((REQS, 1))
    row_index = set_ends(jax.random.randint(seeds[8], (REQS,), 0, NODE_DEV), jax.random.fold_in(seeds[8], 1), 0, NODE_DEV - 1).astype(jnp.int32)
    count_one = set_ends(jax.random.randint(seeds[9], (TGT_DEV * N_FEAT * N_ROWS,), 1, K1 + 1), jax.random.fold_in(seeds[9], 1), 1, K1).astype(jnp.int32)
    neighbours_two = set_ends(jax.random.randint(seeds[10], (TARGETS, K2), 0, TGT_DEV), jax.random.fold_in(seeds[10], 1), 0, TGT_DEV - 1).astype(jnp.int32)
    count_two = set_ends(jax.random.randint(seeds[11], (TARGETS,), 1, K2 + 1), jax.random.fold_in(seeds[11], 1), 1, K2).astype(jnp.int32)
    return dict(features=features, w1_self=w1_self, w1_neigh=w1_neigh, bias_one=bias_one, w2_self=w2_self, w2_neigh=w2_neigh, bias_two=bias_two, owner=owner, row_index=row_index, count_one=count_one, neighbours_two=neighbours_two, count_two=count_two)


def reference(features, w1_self, w1_neigh, bias_one, w2_self, w2_neigh, bias_two, owner, row_index, count_one, neighbours_two, count_two):
    group_targets = TGT_DEV * N_FEAT
    owners = owner[:, 0].reshape(N_ROWS, REQ)
    indices = row_index.reshape(N_ROWS, REQ)
    counts = count_one.reshape(N_ROWS, group_targets)

    def first_layer(packed):
        own, idx, cnt = packed
        rows_read = features[own * NODE_DEV + idx].reshape(group_targets, K1 + 1, F)
        own_rows = rows_read[:, 0]
        neigh = rows_read[:, 1:].astype(jnp.float32)
        valid = (jnp.arange(K1)[None, :] < cnt[:, None]).astype(jnp.float32)
        agg = (jnp.sum(neigh * valid[:, :, None], axis=1) / cnt[:, None].astype(jnp.float32)).astype(jnp.bfloat16)
        pre = jnp.dot(own_rows, w1_self, preferred_element_type=jnp.float32) + jnp.dot(agg, w1_neigh, preferred_element_type=jnp.float32)
        return jax.nn.relu(pre + bias_one).astype(jnp.bfloat16)

    hidden_one = lax.map(first_layer, (owners, indices, counts)).reshape(DEVICES, TGT_DEV, HID)
    blocks = neighbours_two.reshape(DEVICES, TGT_DEV, K2)
    counts_two = count_two.reshape(DEVICES, TGT_DEV)

    def second_layer(packed):
        state, nbr, cnt = packed
        gathered = state[nbr].astype(jnp.float32)
        valid = (jnp.arange(K2)[None, :] < cnt[:, None]).astype(jnp.float32)
        agg = (jnp.sum(gathered * valid[:, :, None], axis=1) / cnt[:, None].astype(jnp.float32)).astype(jnp.bfloat16)
        total = jnp.dot(state, w2_self, preferred_element_type=jnp.float32) + jnp.dot(agg, w2_neigh, preferred_element_type=jnp.float32)
        return (total + bias_two).astype(jnp.bfloat16)

    return lax.map(second_layer, (hidden_one, blocks, counts_two)).reshape(DEVICES * TGT_DEV, HID)
```

```python
import jax
import jax.numpy as jnp
from jax import lax
from jax.experimental import pallas as pl
from jax.experimental.pallas import tpu as pltpu
from jax.sharding import PartitionSpec as P

K1 = 15
K2 = 10
LANES = 128
PEERS = 64
CAPACITY = 80
HALF = CAPACITY // 2
GROUPS = 3
WIDTH = 48
PART = WIDTH // GROUPS
TRIPLES = -(-PEERS // GROUPS)
HIGH = 256
LOWS = 16
BLOCK = 16
VMEM = pltpu.VMEM
LIMIT = 48 * 1024 * 1024
NT = (((1,), (1,)), ((), ()))


def iota(shape, dimension):
    return lax.broadcasted_iota(jnp.int32, shape, dimension)


def route_kernel(owner_ref, row_ref, count_ref, request_ref, code_ref):
    chunks = owner_ref.shape[0]
    mask = owner_ref[...][:, None, :] == iota((chunks, PEERS, LANES), 1)
    ones = jnp.where(mask, 1.0, 0.0)
    before = iota((LANES, 2 * LANES), 0)
    upto = iota((LANES, 2 * LANES), 1)
    prefix = jnp.where((before < upto) | (upto >= LANES), 1.0, 0.0).astype(jnp.bfloat16)
    sums = jnp.dot(
        ones.astype(jnp.bfloat16).reshape(chunks * PEERS, LANES),
        prefix,
        preferred_element_type=jnp.float32,
    ).reshape(chunks, PEERS, 2 * LANES)

    per_chunk = LANES // (K1 + 1)
    half = chunks // 2
    chunk = iota((chunks, LANES), 0)
    lane = iota((chunks, LANES), 1)
    count = count_ref[...].astype(jnp.float32)
    spread = jnp.concatenate(
        [jnp.broadcast_to(count[i : i + 1], (half, LANES)) for i in range(2)], axis=0
    )
    spread = jnp.where(lane // per_chunk == chunk % half, spread, 0.0)
    pick = jnp.where(
        iota((LANES, LANES), 0) % per_chunk == iota((LANES, LANES), 1) // (K1 + 1), 1.0, 0.0
    )
    limit = jnp.dot(
        spread.astype(jnp.bfloat16), pick.astype(jnp.bfloat16), preferred_element_type=jnp.float32
    )
    place = lane % (K1 + 1)
    target = (chunk * per_chunk + lane // (K1 + 1) + 1).astype(jnp.float32)
    code = jnp.where(
        place == 0, -target, jnp.where(place.astype(jnp.float32) <= limit, target, 0.0)
    )
    row = row_ref[...]
    high = (row >> 6).astype(jnp.float32)
    low = (row & 63).astype(jnp.float32)

    offset = jnp.zeros((PEERS, LANES), jnp.float32)
    total = jnp.zeros((3 * PEERS, CAPACITY), jnp.float32)
    slot = iota((CAPACITY, LANES), 0).astype(jnp.float32)
    values, slots = [], []
    for c in range(chunks):
        here = mask[c]
        rank = jnp.sum(
            jnp.where(here, sums[c, :, :LANES] + offset, 0.0), axis=0, keepdims=True
        )
        offset = offset + sums[c, :, LANES:]
        slots.append(jnp.where(slot == rank, 1.0, 0.0).astype(jnp.bfloat16))
        values.append(
            jnp.concatenate(
                [jnp.where(here, v[c : c + 1], 0.0) for v in (high, low, code)], axis=0
            ).astype(jnp.bfloat16)
        )
        if c % 2 == 1:
            total = total + lax.dot_general(
                jnp.concatenate(values, axis=1),
                jnp.concatenate(slots, axis=1),
                NT,
                preferred_element_type=jnp.float32,
            )
            values, slots = [], []
    request_ref[...] = jnp.zeros_like(request_ref)
    code_ref[...] = jnp.zeros_like(code_ref)
    request_ref[:, 0, :CAPACITY] = (
        total[:PEERS] * 64.0 + total[PEERS : 2 * PEERS]
    ).astype(jnp.int32)
    code_ref[:, :CAPACITY] = total[2 * PEERS :]


def spread_halves(slots, scratch):
    lane = iota(slots.shape, 1)

    def pick(parts):
        out = jnp.where(lane < HALF, parts[0], jnp.where(lane < 2 * HALF, parts[1], parts[2]))
        return jnp.where(lane < GROUPS * HALF, out, jnp.zeros_like(out))

    scratch[:, PEERS:, :] = jnp.zeros_like(scratch[:, PEERS:, :])
    scratch[0, :PEERS, :] = pick([slots, pltpu.roll(slots, HALF, 1), pltpu.roll(slots, 2 * HALF, 1)])
    scratch[1, :PEERS, :] = pick([pltpu.roll(slots, LANES - HALF, 1), slots, pltpu.roll(slots, HALF, 1)])


def triple_row(scratch, half, triple):
    lane = iota((1, LANES), 1)
    rows = [scratch[half, pl.ds(GROUPS * triple + x, 1), :] for x in range(GROUPS)]
    return jnp.where(lane < HALF, rows[0], jnp.where(lane < 2 * HALF, rows[1], rows[2]))


def swap_groups(parts):
    lane = iota(parts[0].shape, 1)
    out = []
    for x in range(GROUPS):
        moved = [
            parts[b] if b == x else pltpu.roll(parts[b], (HALF * (b - x)) % LANES, 1)
            for b in range(GROUPS)
        ]
        out.append(
            jnp.where(lane < HALF, moved[0], jnp.where(lane < 2 * HALF, moved[1], moved[2]))
        )
    return out


def find_kernel(asked_ref, features_ref, found_ref, table, scratch):
    spread_halves(asked_ref[:, 0, :], scratch)
    for low in range(LOWS):
        table[low * WIDTH : (low + 1) * WIDTH, :] = features_ref[:, low * HIGH : (low + 1) * HIGH]

    def step(triple, last):
        index = jnp.concatenate([triple_row(scratch, h, triple) for h in range(2)], axis=1)
        chosen = jnp.where(iota((HIGH, 2 * LANES), 0) == (index & (HIGH - 1)), 1.0, 0.0)
        rows = jnp.dot(table[...], chosen.astype(jnp.bfloat16), preferred_element_type=jnp.float32)
        low = index >> 8
        out = jnp.zeros((WIDTH, 2 * LANES), jnp.float32)
        for k in range(LOWS):
            out = jnp.where(low == k, rows[k * WIDTH : (k + 1) * WIDTH], out)
        for h in range(2):
            half = out[:, h * LANES : (h + 1) * LANES]
            tiles = swap_groups([half[b * PART : (b + 1) * PART] for b in range(GROUPS)])
            for x in range(1 if last else GROUPS):
                found_ref[GROUPS * triple + x, h * PART : (h + 1) * PART, :] = tiles[x].astype(
                    jnp.bfloat16
                )

    def body(i, carry):
        for k in range(3):
            step(3 * i + k, False)
        return carry

    lax.fori_loop(0, (TRIPLES - 1) // 3, body, 0)
    step(TRIPLES - 1, True)


def mean_kernel(reply_ref, code_ref, out_ref, scratch, total):
    spread_halves(code_ref[...], scratch)
    targets = out_ref.shape[0]
    total[...] = jnp.zeros_like(total)

    def step(triple, last):
        code = jnp.concatenate([triple_row(scratch, h, triple) for h in range(2)], axis=1)
        row = iota((2 * targets, 2 * LANES), 0)
        wanted = jnp.where(row < targets, -(row + 1), row - targets + 1).astype(jnp.float32)
        member = jnp.where(wanted == code, 1.0, 0.0).astype(jnp.bfloat16)
        halves = []
        for h in range(2):
            tiles = [
                reply_ref[
                    GROUPS * triple + (0 if last else x), h * PART : (h + 1) * PART, :
                ].astype(jnp.float32)
                for x in range(GROUPS)
            ]
            columns = swap_groups(tiles)
            halves.append(
                jnp.concatenate(
                    columns + columns + [jnp.ones((2 * PART, LANES), jnp.float32)], axis=0
                ).astype(jnp.bfloat16)
            )
        total[...] += lax.dot_general(
            member, jnp.concatenate(halves, axis=1), NT, preferred_element_type=jnp.float32
        )

    def body(i, carry):
        for k in range(3):
            step(3 * i + k, False)
        return carry

    lax.fori_loop(0, (TRIPLES - 1) // 3, body, 0)
    step(TRIPLES - 1, True)
    own = total[:targets]
    neigh = total[targets:]
    mean = neigh / neigh[:, 2 * WIDTH : 2 * WIDTH + 1]
    out_ref[...] = jnp.where(iota(own.shape, 1) < WIDTH, own, mean).astype(jnp.bfloat16)


def layers_kernel(
    part_ref,
    w1_self_ref,
    w1_neigh_ref,
    bias_one_ref,
    w2_self_ref,
    w2_neigh_ref,
    bias_two_ref,
    neighbours_ref,
    count_ref,
    out_ref,
):
    parts = [part_ref[i].astype(jnp.float32) for i in range(part_ref.shape[0])]
    own = jnp.concatenate([p[:, :WIDTH] for p in parts], axis=1).astype(jnp.bfloat16)
    mean = jnp.concatenate([p[:, WIDTH : 2 * WIDTH] for p in parts], axis=1).astype(jnp.bfloat16)
    pre = jnp.dot(own, w1_self_ref[...], preferred_element_type=jnp.float32) + jnp.dot(
        mean, w1_neigh_ref[...], preferred_element_type=jnp.float32
    )
    hidden = jnp.maximum(pre + bias_one_ref[...], 0.0).astype(jnp.bfloat16)
    lane = iota((BLOCK, BLOCK), 1)
    count = jnp.sum(
        jnp.where(lane == iota((BLOCK, BLOCK), 0), count_ref[...].astype(jnp.float32), 0.0),
        axis=1,
        keepdims=True,
    )
    member = jnp.zeros((BLOCK, BLOCK), jnp.float32)
    for j in range(K2):
        named = (neighbours_ref[:, j : j + 1] == lane) & (count > j)
        member = member + jnp.where(named, 1.0, 0.0)
    sums = jnp.dot(member.astype(jnp.bfloat16), hidden, preferred_element_type=jnp.float32)
    mean_two = (sums / count).astype(jnp.bfloat16)
    total = jnp.dot(hidden, w2_self_ref[...], preferred_element_type=jnp.float32) + jnp.dot(
        mean_two, w2_neigh_ref[...], preferred_element_type=jnp.float32
    )
    out_ref[...] = (total + bias_two_ref[...]).astype(jnp.bfloat16)


def call(kernel, out_shape, scratch_shapes, *operands):
    return pl.pallas_call(
        kernel,
        out_shape=out_shape,
        in_specs=[pl.BlockSpec(memory_space=VMEM)] * len(operands),
        out_specs=jax.tree.map(lambda _: pl.BlockSpec(memory_space=VMEM), out_shape),
        scratch_shapes=scratch_shapes,
        compiler_params=pltpu.CompilerParams(vmem_limit_bytes=LIMIT),
    )(*operands)


def route(owner, row_index, count_one):
    lines = owner.shape[0] // LANES
    return call(
        route_kernel,
        [
            jax.ShapeDtypeStruct((PEERS, 1, LANES), jnp.int32),
            jax.ShapeDtypeStruct((PEERS, LANES), jnp.float32),
        ],
        [],
        owner.reshape(lines, LANES),
        row_index.reshape(lines, LANES),
        count_one.reshape(-1, LANES),
    )


def find(asked, features):
    return call(
        find_kernel,
        jax.ShapeDtypeStruct((PEERS, 2 * PART, LANES), jnp.bfloat16),
        [
            pltpu.VMEM((LOWS * WIDTH, HIGH), jnp.bfloat16),
            pltpu.VMEM((2, PEERS + 8, LANES), jnp.int32),
        ],
        asked,
        features.T,
    )


def means(replies, code, targets):
    return call(
        mean_kernel,
        jax.ShapeDtypeStruct((targets, LANES), jnp.bfloat16),
        [
            pltpu.VMEM((2, PEERS + 8, LANES), jnp.float32),
            pltpu.VMEM((2 * targets, LANES), jnp.float32),
        ],
        replies,
        code,
    )


def layers(parts, w1_self, w1_neigh, bias_one, w2_self, w2_neigh, bias_two, neighbours, count):
    return call(
        layers_kernel,
        jax.ShapeDtypeStruct((BLOCK, w2_self.shape[1]), jnp.bfloat16),
        [],
        parts,
        w1_self,
        w1_neigh,
        bias_one.reshape(1, -1),
        w2_self,
        w2_neigh,
        bias_two.reshape(1, -1),
        neighbours,
        count.reshape(1, -1),
    )


def per_device(
    features,
    w1_self,
    w1_neigh,
    bias_one,
    w2_self,
    w2_neigh,
    bias_two,
    owner,
    row_index,
    count_one,
    neighbours_two,
    count_two,
):
    requests, code = route(owner, row_index, count_one)
    asked = lax.all_to_all(requests, "rows", split_axis=0, concat_axis=0, tiled=True)
    found = find(asked, features)
    replies = lax.all_to_all(found, "rows", split_axis=0, concat_axis=0, tiled=True)
    mine = means(replies, code, count_one.shape[0])
    mine = mine.reshape(-1, BLOCK, LANES)
    parts = lax.all_to_all(mine, "feat", split_axis=0, concat_axis=0, tiled=True)
    return layers(
        parts, w1_self, w1_neigh, bias_one, w2_self, w2_neigh, bias_two, neighbours_two, count_two
    )


def solution(mesh):
    return jax.shard_map(
        per_device,
        mesh=mesh,
        in_specs=(
            P("rows", "feat"),
            P(),
            P(),
            P(),
            P(),
            P(),
            P(),
            P("rows", None),
            P("rows"),
            P("rows"),
            P(("rows", "feat"), None),
            P(("rows", "feat")),
        ),
        out_specs=P(("rows", "feat"), None),
        check_vma=False,
    )
```

```python
import jax
import jax.numpy as jnp
from jax import lax
from jax.experimental import pallas as pl
from jax.experimental.pallas import tpu as pltpu
from jax.sharding import PartitionSpec as P

K1 = 15
K2 = 10
LANES = 128
PEERS = 64
CAPACITY = 80
HALF = CAPACITY // 2
GROUPS = 3
WIDTH = 48
PART = WIDTH // GROUPS
TRIPLES = -(-PEERS // GROUPS)
HIGH = 256
LOWS = 16
BLOCK = 16
VMEM = pltpu.VMEM
LIMIT = 12 * 1024 * 1024
NT = (((1,), (1,)), ((), ()))


def iota(shape, dimension):
    return lax.broadcasted_iota(jnp.int32, shape, dimension)


def route_kernel(
    owner_hbm, row_hbm, count_hbm, request_ref, code_ref, owner_ref, row_ref, count_ref, arrived
):
    copies = [
        pltpu.make_async_copy(source, target, arrived.at[i])
        for i, (source, target) in enumerate(
            ((owner_hbm, owner_ref), (row_hbm, row_ref), (count_hbm, count_ref))
        )
    ]
    for copy in copies:
        copy.start()
    for copy in copies:
        copy.wait()
    chunks = owner_ref.shape[0]
    mask = owner_ref[...][:, None, :] == iota((chunks, PEERS, LANES), 1)
    ones = jnp.where(mask, 1.0, 0.0)
    before = iota((LANES, 2 * LANES), 0)
    upto = iota((LANES, 2 * LANES), 1)
    prefix = jnp.where((before < upto) | (upto >= LANES), 1.0, 0.0).astype(jnp.bfloat16)
    sums = jnp.dot(
        ones.astype(jnp.bfloat16).reshape(chunks * PEERS, LANES),
        prefix,
        preferred_element_type=jnp.float32,
    ).reshape(chunks, PEERS, 2 * LANES)

    per_chunk = LANES // (K1 + 1)
    half = chunks // 2
    chunk = iota((chunks, LANES), 0)
    lane = iota((chunks, LANES), 1)
    count = count_ref[...].astype(jnp.float32)
    spread = jnp.concatenate(
        [jnp.broadcast_to(count[i : i + 1], (half, LANES)) for i in range(2)], axis=0
    )
    spread = jnp.where(lane // per_chunk == chunk % half, spread, 0.0)
    pick = jnp.where(
        iota((LANES, LANES), 0) % per_chunk == iota((LANES, LANES), 1) // (K1 + 1), 1.0, 0.0
    )
    limit = jnp.dot(
        spread.astype(jnp.bfloat16), pick.astype(jnp.bfloat16), preferred_element_type=jnp.float32
    )
    place = lane % (K1 + 1)
    target = (chunk * per_chunk + lane // (K1 + 1) + 1).astype(jnp.float32)
    code = jnp.where(
        place == 0, -target, jnp.where(place.astype(jnp.float32) <= limit, target, 0.0)
    )
    row = row_ref[...]
    high = (row >> 6).astype(jnp.float32)
    low = (row & 63).astype(jnp.float32)

    offset = jnp.zeros((PEERS, LANES), jnp.float32)
    total = jnp.zeros((3 * PEERS, CAPACITY), jnp.float32)
    slot = iota((CAPACITY, LANES), 0).astype(jnp.float32)
    values, slots = [], []
    for c in range(chunks):
        here = mask[c]
        rank = jnp.sum(
            jnp.where(here, sums[c, :, :LANES] + offset, 0.0), axis=0, keepdims=True
        )
        offset = offset + sums[c, :, LANES:]
        slots.append(jnp.where(slot == rank, 1.0, 0.0).astype(jnp.bfloat16))
        values.append(
            jnp.concatenate(
                [jnp.where(here, v[c : c + 1], 0.0) for v in (high, low, code)], axis=0
            ).astype(jnp.bfloat16)
        )
        if c % 2 == 1:
            total = total + lax.dot_general(
                jnp.concatenate(values, axis=1),
                jnp.concatenate(slots, axis=1),
                NT,
                preferred_element_type=jnp.float32,
            )
            values, slots = [], []
    request_ref[...] = jnp.zeros_like(request_ref)
    code_ref[...] = jnp.zeros_like(code_ref)
    request_ref[:, 0, :CAPACITY] = (
        total[:PEERS] * 64.0 + total[PEERS : 2 * PEERS]
    ).astype(jnp.int32)
    code_ref[:, :CAPACITY] = total[2 * PEERS :]


def spread_halves(slots, scratch):
    lane = iota(slots.shape, 1)

    def pick(parts):
        out = jnp.where(lane < HALF, parts[0], jnp.where(lane < 2 * HALF, parts[1], parts[2]))
        return jnp.where(lane < GROUPS * HALF, out, jnp.zeros_like(out))

    scratch[:, PEERS:, :] = jnp.zeros_like(scratch[:, PEERS:, :])
    scratch[0, :PEERS, :] = pick([slots, pltpu.roll(slots, HALF, 1), pltpu.roll(slots, 2 * HALF, 1)])
    scratch[1, :PEERS, :] = pick([pltpu.roll(slots, LANES - HALF, 1), slots, pltpu.roll(slots, HALF, 1)])


def triple_row(scratch, half, triple):
    lane = iota((1, LANES), 1)
    rows = [scratch[half, pl.ds(GROUPS * triple + x, 1), :] for x in range(GROUPS)]
    return jnp.where(lane < HALF, rows[0], jnp.where(lane < 2 * HALF, rows[1], rows[2]))


def swap_groups(parts):
    lane = iota(parts[0].shape, 1)
    out = []
    for x in range(GROUPS):
        moved = [
            parts[b] if b == x else pltpu.roll(parts[b], (HALF * (b - x)) % LANES, 1)
            for b in range(GROUPS)
        ]
        out.append(
            jnp.where(lane < HALF, moved[0], jnp.where(lane < 2 * HALF, moved[1], moved[2]))
        )
    return out


def find_kernel(asked_ref, features_ref, found_ref, table, scratch):
    spread_halves(asked_ref[:, 0, :], scratch)
    for low in range(LOWS):
        table[low * WIDTH : (low + 1) * WIDTH, :] = features_ref[:, low * HIGH : (low + 1) * HIGH]

    def step(triple, last):
        index = jnp.concatenate([triple_row(scratch, h, triple) for h in range(2)], axis=1)
        chosen = jnp.where(iota((HIGH, 2 * LANES), 0) == (index & (HIGH - 1)), 1.0, 0.0)
        rows = jnp.dot(table[...], chosen.astype(jnp.bfloat16), preferred_element_type=jnp.float32)
        low = index >> 8
        out = jnp.zeros((WIDTH, 2 * LANES), jnp.float32)
        for k in range(LOWS):
            out = jnp.where(low == k, rows[k * WIDTH : (k + 1) * WIDTH], out)
        for h in range(2):
            half = out[:, h * LANES : (h + 1) * LANES]
            tiles = swap_groups([half[b * PART : (b + 1) * PART] for b in range(GROUPS)])
            for x in range(1 if last else GROUPS):
                found_ref[GROUPS * triple + x, h * PART : (h + 1) * PART, :] = tiles[x].astype(
                    jnp.bfloat16
                )

    def body(i, carry):
        for k in range(3):
            step(3 * i + k, False)
        return carry

    lax.fori_loop(0, (TRIPLES - 1) // 3, body, 0)
    step(TRIPLES - 1, True)


def mean_kernel(reply_ref, code_ref, out_ref, scratch, total):
    spread_halves(code_ref[...], scratch)
    targets = out_ref.shape[0]
    total[...] = jnp.zeros_like(total)

    def step(triple, last):
        code = jnp.concatenate([triple_row(scratch, h, triple) for h in range(2)], axis=1)
        row = iota((2 * targets, 2 * LANES), 0)
        wanted = jnp.where(row < targets, -(row + 1), row - targets + 1).astype(jnp.float32)
        member = jnp.where(wanted == code, 1.0, 0.0).astype(jnp.bfloat16)
        halves = []
        for h in range(2):
            tiles = [
                reply_ref[
                    GROUPS * triple + (0 if last else x), h * PART : (h + 1) * PART, :
                ].astype(jnp.float32)
                for x in range(GROUPS)
            ]
            columns = swap_groups(tiles)
            halves.append(
                jnp.concatenate(
                    columns + columns + [jnp.ones((2 * PART, LANES), jnp.float32)], axis=0
                ).astype(jnp.bfloat16)
            )
        total[...] += lax.dot_general(
            member, jnp.concatenate(halves, axis=1), NT, preferred_element_type=jnp.float32
        )

    def body(i, carry):
        for k in range(3):
            step(3 * i + k, False)
        return carry

    lax.fori_loop(0, (TRIPLES - 1) // 3, body, 0)
    step(TRIPLES - 1, True)
    own = total[:targets]
    neigh = total[targets:]
    mean = neigh / neigh[:, 2 * WIDTH : 2 * WIDTH + 1]
    out_ref[...] = jnp.where(iota(own.shape, 1) < WIDTH, own, mean).astype(jnp.bfloat16)


def layers_kernel(
    part_ref,
    w1_self_ref,
    w1_neigh_ref,
    bias_one_ref,
    w2_self_ref,
    w2_neigh_ref,
    bias_two_ref,
    neighbours_ref,
    count_ref,
    out_ref,
):
    parts = [part_ref[i].astype(jnp.float32) for i in range(part_ref.shape[0])]
    own = jnp.concatenate([p[:, :WIDTH] for p in parts], axis=1).astype(jnp.bfloat16)
    mean = jnp.concatenate([p[:, WIDTH : 2 * WIDTH] for p in parts], axis=1).astype(jnp.bfloat16)
    pre = jnp.dot(own, w1_self_ref[...], preferred_element_type=jnp.float32) + jnp.dot(
        mean, w1_neigh_ref[...], preferred_element_type=jnp.float32
    )
    hidden = jnp.maximum(pre + bias_one_ref[...], 0.0).astype(jnp.bfloat16)
    lane = iota((BLOCK, BLOCK), 1)
    count = jnp.sum(
        jnp.where(lane == iota((BLOCK, BLOCK), 0), count_ref[...].astype(jnp.float32), 0.0),
        axis=1,
        keepdims=True,
    )
    member = jnp.zeros((BLOCK, BLOCK), jnp.float32)
    for j in range(K2):
        named = (neighbours_ref[:, j : j + 1] == lane) & (count > j)
        member = member + jnp.where(named, 1.0, 0.0)
    sums = jnp.dot(member.astype(jnp.bfloat16), hidden, preferred_element_type=jnp.float32)
    mean_two = (sums / count).astype(jnp.bfloat16)
    total = jnp.dot(hidden, w2_self_ref[...], preferred_element_type=jnp.float32) + jnp.dot(
        mean_two, w2_neigh_ref[...], preferred_element_type=jnp.float32
    )
    out_ref[...] = (total + bias_two_ref[...]).astype(jnp.bfloat16)


def call(kernel, out_shape, scratch_shapes, flops, *operands, space=VMEM):
    return pl.pallas_call(
        kernel,
        out_shape=out_shape,
        in_specs=[pl.BlockSpec(memory_space=space)] * len(operands),
        out_specs=jax.tree.map(lambda _: pl.BlockSpec(memory_space=VMEM), out_shape),
        scratch_shapes=scratch_shapes,
        compiler_params=pltpu.CompilerParams(vmem_limit_bytes=LIMIT),
        cost_estimate=pl.CostEstimate(flops=flops, bytes_accessed=1 << 20, transcendentals=0),
    )(*operands)


def route(owner, row_index, count_one):
    lines = owner.shape[0] // LANES
    return call(
        route_kernel,
        [
            jax.ShapeDtypeStruct((PEERS, 1, LANES), jnp.int32),
            jax.ShapeDtypeStruct((PEERS, LANES), jnp.float32),
        ],
        [
            pltpu.VMEM((lines, LANES), jnp.int32),
            pltpu.VMEM((lines, LANES), jnp.int32),
            pltpu.VMEM((count_one.shape[0] // LANES, LANES), jnp.int32),
            pltpu.SemaphoreType.DMA((3,)),
        ],
        1 << 30,
        *[
            pltpu.with_memory_space_constraint(a.reshape(-1, LANES), pltpu.HBM)
            for a in (owner, row_index, count_one)
        ],
        space=pltpu.HBM,
    )


def find(asked, features):
    return call(
        find_kernel,
        jax.ShapeDtypeStruct((PEERS, 2 * PART, LANES), jnp.bfloat16),
        [
            pltpu.VMEM((LOWS * WIDTH, HIGH), jnp.bfloat16),
            pltpu.VMEM((2, PEERS + 8, LANES), jnp.int32),
        ],
        5 << 30,
        asked,
        features.T,
    )


def means(replies, code, targets):
    return call(
        mean_kernel,
        jax.ShapeDtypeStruct((targets, LANES), jnp.bfloat16),
        [
            pltpu.VMEM((2, PEERS + 8, LANES), jnp.float32),
            pltpu.VMEM((2 * targets, LANES), jnp.float32),
        ],
        4 << 30,
        replies,
        code,
    )


def layers(parts, w1_self, w1_neigh, bias_one, w2_self, w2_neigh, bias_two, neighbours, count):
    return call(
        layers_kernel,
        jax.ShapeDtypeStruct((BLOCK, w2_self.shape[1]), jnp.bfloat16),
        [],
        3 << 30,
        parts,
        w1_self,
        w1_neigh,
        bias_one.reshape(1, -1),
        w2_self,
        w2_neigh,
        bias_two.reshape(1, -1),
        neighbours,
        count.reshape(1, -1),
    )


def per_device(
    features,
    w1_self,
    w1_neigh,
    bias_one,
    w2_self,
    w2_neigh,
    bias_two,
    owner,
    row_index,
    count_one,
    neighbours_two,
    count_two,
):
    requests, code = route(owner, row_index, count_one)
    asked = lax.all_to_all(requests, "rows", split_axis=0, concat_axis=0, tiled=True)
    found = find(asked, features)
    replies = lax.all_to_all(found, "rows", split_axis=0, concat_axis=0, tiled=True)
    mine = means(replies, code, count_one.shape[0])
    mine = mine.reshape(-1, BLOCK, LANES)
    parts = lax.all_to_all(mine, "feat", split_axis=0, concat_axis=0, tiled=True)
    return layers(
        parts, w1_self, w1_neigh, bias_one, w2_self, w2_neigh, bias_two, neighbours_two, count_two
    )


def solution(mesh):
    return jax.shard_map(
        per_device,
        mesh=mesh,
        in_specs=(
            P("rows", "feat"),
            P(),
            P(),
            P(),
            P(),
            P(),
            P(),
            P("rows", None),
            P("rows"),
            P("rows"),
            P(("rows", "feat"), None),
            P(("rows", "feat")),
        ),
        out_specs=P(("rows", "feat"), None),
        check_vma=False,
    )
```

```python
import jax
import jax.numpy as jnp
from jax import lax
from jax.experimental import pallas as pl
from jax.experimental.pallas import tpu as pltpu
from jax.sharding import PartitionSpec as P

K1 = 15
K2 = 10
LANES = 128
PEERS = 64
CAPACITY = 80
HALF = CAPACITY // 2
GROUPS = 3
WIDTH = 48
PART = WIDTH // GROUPS
TRIPLES = -(-PEERS // GROUPS)
HIGH = 512
PLANE = 256
LOWS = 8
BLOCK = 16
VMEM = pltpu.VMEM
LIMIT = 12 * 1024 * 1024
NT = (((1,), (1,)), ((), ()))


def iota(shape, dimension):
    return lax.broadcasted_iota(jnp.int32, shape, dimension)


def route_kernel(
    owner_hbm, row_hbm, count_hbm, request_ref, code_ref, owner_ref, row_ref, count_ref, arrived
):
    copies = [
        pltpu.make_async_copy(source, target, arrived.at[i])
        for i, (source, target) in enumerate(
            ((owner_hbm, owner_ref), (row_hbm, row_ref), (count_hbm, count_ref))
        )
    ]
    for copy in copies:
        copy.start()
    for copy in copies:
        copy.wait()
    chunks = owner_ref.shape[0]
    mask = owner_ref[...][:, None, :] == iota((chunks, PEERS, LANES), 1)
    ones = jnp.where(mask, 1.0, 0.0)
    before = iota((LANES, 2 * LANES), 0)
    upto = iota((LANES, 2 * LANES), 1)
    prefix = jnp.where((before < upto) | (upto >= LANES), 1.0, 0.0).astype(jnp.bfloat16)
    sums = jnp.dot(
        ones.astype(jnp.bfloat16).reshape(chunks * PEERS, LANES),
        prefix,
        preferred_element_type=jnp.float32,
    ).reshape(chunks, PEERS, 2 * LANES)

    per_chunk = LANES // (K1 + 1)
    half = chunks // 2
    chunk = iota((chunks, LANES), 0)
    lane = iota((chunks, LANES), 1)
    count = count_ref[...].astype(jnp.float32)
    spread = jnp.concatenate(
        [jnp.broadcast_to(count[i : i + 1], (half, LANES)) for i in range(2)], axis=0
    )
    spread = jnp.where(lane // per_chunk == chunk % half, spread, 0.0)
    pick = jnp.where(
        iota((LANES, LANES), 0) % per_chunk == iota((LANES, LANES), 1) // (K1 + 1), 1.0, 0.0
    )
    limit = jnp.dot(
        spread.astype(jnp.bfloat16), pick.astype(jnp.bfloat16), preferred_element_type=jnp.float32
    )
    place = lane % (K1 + 1)
    target = (chunk * per_chunk + lane // (K1 + 1) + 1).astype(jnp.float32)
    code = jnp.where(
        place == 0, -target, jnp.where(place.astype(jnp.float32) <= limit, target, 0.0)
    )
    row = row_ref[...]
    high = (row >> 6).astype(jnp.float32)
    low = (row & 63).astype(jnp.float32)

    offset = jnp.zeros((PEERS, LANES), jnp.float32)
    total = jnp.zeros((3 * PEERS, CAPACITY), jnp.float32)
    slot = iota((CAPACITY, LANES), 0).astype(jnp.float32)
    values, slots = [], []
    for c in range(chunks):
        here = mask[c]
        rank = jnp.sum(
            jnp.where(here, sums[c, :, :LANES] + offset, 0.0), axis=0, keepdims=True
        )
        offset = offset + sums[c, :, LANES:]
        slots.append(jnp.where(slot == rank, 1.0, 0.0).astype(jnp.bfloat16))
        values.append(
            jnp.concatenate(
                [jnp.where(here, v[c : c + 1], 0.0) for v in (high, low, code)], axis=0
            ).astype(jnp.bfloat16)
        )
        if c % 2 == 1:
            total = total + lax.dot_general(
                jnp.concatenate(values, axis=1),
                jnp.concatenate(slots, axis=1),
                NT,
                preferred_element_type=jnp.float32,
            )
            values, slots = [], []
    request_ref[...] = jnp.zeros_like(request_ref)
    code_ref[...] = jnp.zeros_like(code_ref)
    request_ref[:, 0, :CAPACITY] = (
        total[:PEERS] * 64.0 + total[PEERS : 2 * PEERS]
    ).astype(jnp.int32)
    code_ref[:, :CAPACITY] = total[2 * PEERS :]


def spread_halves(slots, scratch):
    lane = iota(slots.shape, 1)

    def pick(parts):
        out = jnp.where(lane < HALF, parts[0], jnp.where(lane < 2 * HALF, parts[1], parts[2]))
        return jnp.where(lane < GROUPS * HALF, out, jnp.zeros_like(out))

    scratch[:, PEERS:, :] = jnp.zeros_like(scratch[:, PEERS:, :])
    scratch[0, :PEERS, :] = pick([slots, pltpu.roll(slots, HALF, 1), pltpu.roll(slots, 2 * HALF, 1)])
    scratch[1, :PEERS, :] = pick([pltpu.roll(slots, LANES - HALF, 1), slots, pltpu.roll(slots, HALF, 1)])


def triple_row(scratch, half, triple):
    lane = iota((1, LANES), 1)
    rows = [scratch[half, pl.ds(GROUPS * triple + x, 1), :] for x in range(GROUPS)]
    return jnp.where(lane < HALF, rows[0], jnp.where(lane < 2 * HALF, rows[1], rows[2]))


def swap_groups(parts):
    lane = iota(parts[0].shape, 1)
    out = []
    for x in range(GROUPS):
        moved = [
            parts[b] if b == x else pltpu.roll(parts[b], (HALF * (b - x)) % LANES, 1)
            for b in range(GROUPS)
        ]
        out.append(
            jnp.where(lane < HALF, moved[0], jnp.where(lane < 2 * HALF, moved[1], moved[2]))
        )
    return out


def find_kernel(asked_ref, features_ref, found_ref, table, scratch):
    spread_halves(asked_ref[:, 0, :], scratch)
    for low in range(LOWS):
        table[low * WIDTH : (low + 1) * WIDTH, :] = features_ref[:, low * HIGH : (low + 1) * HIGH]
    one = jnp.bfloat16(1.0)
    zero = jnp.bfloat16(0.0)
    number = iota((PLANE, 2 * LANES), 0).astype(jnp.float32).astype(jnp.bfloat16)

    def step(triple, last):
        index = jnp.concatenate([triple_row(scratch, h, triple) for h in range(2)], axis=1)
        chosen = []
        for k in range(HIGH // PLANE):
            here = (index >> 8) & (HIGH // PLANE - 1)
            key = jnp.where(here == k, index & (PLANE - 1), -1).astype(jnp.float32).astype(jnp.bfloat16)
            chosen.append(jnp.where(number == key, one, zero))
        chosen = jnp.concatenate(chosen, axis=0) if len(chosen) > 1 else chosen[0]
        rows = jnp.dot(table[...], chosen, preferred_element_type=jnp.float32)
        low = index // HIGH
        out = rows[:WIDTH]
        for k in range(1, LOWS):
            out = jnp.where(low == k, rows[k * WIDTH : (k + 1) * WIDTH], out)
        out = out.astype(jnp.bfloat16)
        for h in range(2):
            half = out[:, h * LANES : (h + 1) * LANES]
            tiles = swap_groups([half[b * PART : (b + 1) * PART] for b in range(GROUPS)])
            for x in range(1 if last else GROUPS):
                found_ref[GROUPS * triple + x, h * PART : (h + 1) * PART, :] = tiles[x]

    for triple in range(TRIPLES):
        step(triple, triple == TRIPLES - 1)


def mean_kernel(reply_ref, code_ref, out_ref, scratch):
    spread_halves(code_ref[...], scratch)
    targets = out_ref.shape[0]
    row = iota((2 * targets, 2 * LANES), 0)
    wanted = jnp.where(row < targets, -(row + 1), row - targets + 1)
    wanted = wanted.astype(jnp.float32).astype(jnp.bfloat16)
    one = jnp.bfloat16(1.0)
    zero = jnp.bfloat16(0.0)

    def step(triple, last):
        code = jnp.concatenate([triple_row(scratch, h, triple) for h in range(2)], axis=1)
        member = jnp.where(wanted == code.astype(jnp.bfloat16), one, zero)
        halves = []
        for h in range(2):
            tiles = [
                reply_ref[GROUPS * triple + (0 if last else x), h * PART : (h + 1) * PART, :]
                for x in range(GROUPS)
            ]
            columns = swap_groups(tiles)
            halves.append(
                jnp.concatenate(columns + columns + [jnp.ones((2 * PART, LANES), jnp.bfloat16)], axis=0)
            )
        return member, jnp.concatenate(halves, axis=1)

    def add(parts):
        members = jnp.concatenate([p[0] for p in parts], axis=1)
        columns = jnp.concatenate([p[1] for p in parts], axis=1)
        return lax.dot_general(members, columns, NT, preferred_element_type=jnp.float32)

    sums = add([step(i, i == TRIPLES - 1) for i in range(TRIPLES)])
    own = sums[:targets]
    neigh = sums[targets:]
    mean = neigh / neigh[:, 2 * WIDTH : 2 * WIDTH + 1]
    out_ref[...] = jnp.where(iota(own.shape, 1) < WIDTH, own, mean).astype(jnp.bfloat16)


def layers_kernel(
    part_ref,
    w1_self_ref,
    w1_neigh_ref,
    bias_one_ref,
    w2_self_ref,
    w2_neigh_ref,
    bias_two_ref,
    neighbours_ref,
    count_ref,
    out_ref,
):
    parts = [part_ref[i].astype(jnp.float32) for i in range(part_ref.shape[0])]
    own = jnp.concatenate([p[:, :WIDTH] for p in parts], axis=1).astype(jnp.bfloat16)
    mean = jnp.concatenate([p[:, WIDTH : 2 * WIDTH] for p in parts], axis=1).astype(jnp.bfloat16)
    pre = jnp.dot(own, w1_self_ref[...], preferred_element_type=jnp.float32) + jnp.dot(
        mean, w1_neigh_ref[...], preferred_element_type=jnp.float32
    )
    hidden = jnp.maximum(pre + bias_one_ref[...], 0.0).astype(jnp.bfloat16)
    lane = iota((BLOCK, BLOCK), 1)
    count = jnp.sum(
        jnp.where(lane == iota((BLOCK, BLOCK), 0), count_ref[...].astype(jnp.float32), 0.0),
        axis=1,
        keepdims=True,
    )
    member = jnp.zeros((BLOCK, BLOCK), jnp.float32)
    for j in range(K2):
        named = (neighbours_ref[:, j : j + 1] == lane) & (count > j)
        member = member + jnp.where(named, 1.0, 0.0)
    sums = jnp.dot(member.astype(jnp.bfloat16), hidden, preferred_element_type=jnp.float32)
    mean_two = (sums / count).astype(jnp.bfloat16)
    total = jnp.dot(hidden, w2_self_ref[...], preferred_element_type=jnp.float32) + jnp.dot(
        mean_two, w2_neigh_ref[...], preferred_element_type=jnp.float32
    )
    out_ref[...] = (total + bias_two_ref[...]).astype(jnp.bfloat16)


def call(kernel, out_shape, scratch_shapes, flops, *operands, space=VMEM):
    return pl.pallas_call(
        kernel,
        out_shape=out_shape,
        in_specs=[pl.BlockSpec(memory_space=space)] * len(operands),
        out_specs=jax.tree.map(lambda _: pl.BlockSpec(memory_space=VMEM), out_shape),
        scratch_shapes=scratch_shapes,
        compiler_params=pltpu.CompilerParams(vmem_limit_bytes=LIMIT),
        cost_estimate=pl.CostEstimate(flops=flops, bytes_accessed=1 << 20, transcendentals=0),
    )(*operands)


def route(owner, row_index, count_one):
    lines = owner.shape[0] // LANES
    return call(
        route_kernel,
        [
            jax.ShapeDtypeStruct((PEERS, 1, LANES), jnp.int32),
            jax.ShapeDtypeStruct((PEERS, LANES), jnp.float32),
        ],
        [
            pltpu.VMEM((lines, LANES), jnp.int32),
            pltpu.VMEM((lines, LANES), jnp.int32),
            pltpu.VMEM((count_one.shape[0] // LANES, LANES), jnp.int32),
            pltpu.SemaphoreType.DMA((3,)),
        ],
        1 << 30,
        *[
            pltpu.with_memory_space_constraint(a.reshape(-1, LANES), pltpu.HBM)
            for a in (owner, row_index, count_one)
        ],
        space=pltpu.HBM,
    )


def find(asked, features):
    return call(
        find_kernel,
        jax.ShapeDtypeStruct((PEERS, 2 * PART, LANES), jnp.bfloat16),
        [
            pltpu.VMEM((LOWS * WIDTH, HIGH), jnp.bfloat16),
            pltpu.VMEM((2, PEERS + 8, LANES), jnp.int32),
        ],
        5 << 30,
        asked,
        features.T,
    )


def means(replies, code, targets):
    return call(
        mean_kernel,
        jax.ShapeDtypeStruct((targets, LANES), jnp.bfloat16),
        [
            pltpu.VMEM((2, PEERS + 8, LANES), jnp.float32),
        ],
        4 << 30,
        replies,
        code,
    )


def layers(parts, w1_self, w1_neigh, bias_one, w2_self, w2_neigh, bias_two, neighbours, count):
    return call(
        layers_kernel,
        jax.ShapeDtypeStruct((BLOCK, w2_self.shape[1]), jnp.bfloat16),
        [],
        3 << 30,
        parts,
        w1_self,
        w1_neigh,
        bias_one.reshape(1, -1),
        w2_self,
        w2_neigh,
        bias_two.reshape(1, -1),
        neighbours,
        count.reshape(1, -1),
    )


def per_device(
    features,
    w1_self,
    w1_neigh,
    bias_one,
    w2_self,
    w2_neigh,
    bias_two,
    owner,
    row_index,
    count_one,
    neighbours_two,
    count_two,
):
    requests, code = route(owner, row_index, count_one)
    asked = lax.all_to_all(requests, "rows", split_axis=0, concat_axis=0, tiled=True)
    found = find(asked, features)
    replies = lax.all_to_all(found, "rows", split_axis=0, concat_axis=0, tiled=True)
    mine = means(replies, code, count_one.shape[0])
    mine = mine.reshape(-1, BLOCK, LANES)
    parts = lax.all_to_all(mine, "feat", split_axis=0, concat_axis=0, tiled=True)
    return layers(
        parts, w1_self, w1_neigh, bias_one, w2_self, w2_neigh, bias_two, neighbours_two, count_two
    )


def solution(mesh):
    return jax.shard_map(
        per_device,
        mesh=mesh,
        in_specs=(
            P("rows", "feat"),
            P(),
            P(),
            P(),
            P(),
            P(),
            P(),
            P("rows", None),
            P("rows"),
            P("rows"),
            P(("rows", "feat"), None),
            P(("rows", "feat")),
        ),
        out_specs=P(("rows", "feat"), None),
        check_vma=False,
    )
```

```python
import jax
import jax.numpy as jnp
from jax import lax
from jax.experimental import pallas as pl
from jax.experimental.pallas import tpu as pltpu
from jax.sharding import PartitionSpec as P

K1 = 15
K2 = 10
LANES = 128
PEERS = 64
CAPACITY = 80
USUAL = 64
FLAG = LANES - 1
WIDTH = 48
PART = WIDTH // 2
HIGH = 512
PLANE = 256
LOWS = 8
BLOCK = 16
VMEM = pltpu.VMEM
LIMIT = 12 * 1024 * 1024
NT = (((1,), (1,)), ((), ()))


def iota(shape, dimension):
    return lax.broadcasted_iota(jnp.int32, shape, dimension)


def route_kernel(
    owner_hbm, row_hbm, count_hbm, request_ref, code_ref, owner_ref, row_ref, count_ref, arrived
):
    copies = [
        pltpu.make_async_copy(source, target, arrived.at[i])
        for i, (source, target) in enumerate(
            ((owner_hbm, owner_ref), (row_hbm, row_ref), (count_hbm, count_ref))
        )
    ]
    for copy in copies:
        copy.start()
    for copy in copies:
        copy.wait()
    chunks = owner_ref.shape[0]
    per_chunk = LANES // (K1 + 1)
    half = chunks // 2
    chunk = iota((chunks, LANES), 0)
    lane = iota((chunks, LANES), 1)
    count = count_ref[...].astype(jnp.float32)
    spread = jnp.concatenate(
        [jnp.broadcast_to(count[i : i + 1], (half, LANES)) for i in range(2)], axis=0
    )
    spread = jnp.where(lane // per_chunk == chunk % half, spread, 0.0)
    pick = jnp.where(
        iota((LANES, LANES), 0) % per_chunk == iota((LANES, LANES), 1) // (K1 + 1), 1.0, 0.0
    )
    limit = jnp.dot(
        spread.astype(jnp.bfloat16), pick.astype(jnp.bfloat16), preferred_element_type=jnp.float32
    )
    place = lane % (K1 + 1)
    target = (chunk * per_chunk + lane // (K1 + 1) + 1).astype(jnp.float32)
    code = jnp.where(
        place == 0, -target, jnp.where(place.astype(jnp.float32) <= limit, target, 0.0)
    )
    owner = jnp.where(code == 0.0, -1, owner_ref[...])
    mask = owner[:, None, :] == iota((chunks, PEERS, LANES), 1)
    ones = jnp.where(mask, 1.0, 0.0)
    before = iota((LANES, 2 * LANES), 0)
    upto = iota((LANES, 2 * LANES), 1)
    prefix = jnp.where((before < upto) | (upto >= LANES), 1.0, 0.0).astype(jnp.bfloat16)
    sums = jnp.dot(
        ones.astype(jnp.bfloat16).reshape(chunks * PEERS, LANES),
        prefix,
        preferred_element_type=jnp.float32,
    ).reshape(chunks, PEERS, 2 * LANES)

    row = row_ref[...]
    high = (row >> 6).astype(jnp.float32)
    low = (row & 63).astype(jnp.float32)

    offset = jnp.zeros((PEERS, LANES), jnp.float32)
    total = jnp.zeros((3 * PEERS, CAPACITY), jnp.float32)
    slot = iota((CAPACITY, LANES), 0).astype(jnp.float32)
    values, slots = [], []
    for c in range(chunks):
        here = mask[c]
        rank = jnp.sum(
            jnp.where(here, sums[c, :, :LANES] + offset, 0.0), axis=0, keepdims=True
        )
        offset = offset + sums[c, :, LANES:]
        slots.append(jnp.where(slot == rank, 1.0, 0.0).astype(jnp.bfloat16))
        values.append(
            jnp.concatenate(
                [jnp.where(here, v[c : c + 1], 0.0) for v in (high, low, code)], axis=0
            ).astype(jnp.bfloat16)
        )
        if c % 2 == 1:
            total = total + lax.dot_general(
                jnp.concatenate(values, axis=1),
                jnp.concatenate(slots, axis=1),
                NT,
                preferred_element_type=jnp.float32,
            )
            values, slots = [], []
    crowded = jnp.where(jnp.max(offset) > USUAL, 1, 0)
    request_ref[...] = jnp.where(iota(request_ref.shape, 2) == FLAG, crowded, 0)
    code_ref[...] = jnp.zeros_like(code_ref)
    request_ref[:, 0, :CAPACITY] = (
        total[:PEERS] * 64.0 + total[PEERS : 2 * PEERS]
    ).astype(jnp.int32)
    code_ref[:, :CAPACITY] = total[2 * PEERS :]


def spread(slots, scratch):
    lane = iota(slots.shape, 1)
    scratch[...] = jnp.where(lane < USUAL, slots, pltpu.roll(slots, USUAL, 1))


def two_peers(scratch, peer):
    lane = iota((1, LANES), 1)
    return jnp.where(lane < USUAL, scratch[peer : peer + 1, :], scratch[peer + 1 : peer + 2, :])


def swap(first, second):
    lane = iota(first.shape, 1)
    return (
        jnp.where(lane < USUAL, first, pltpu.roll(second, USUAL, 1)),
        jnp.where(lane < USUAL, pltpu.roll(first, USUAL, 1), second),
    )


def find_kernel(asked_ref, features_ref, found_ref, crowded_ref, table, scratch):
    asked = asked_ref[:, 0, :]
    crowded_ref[0, 0] = jnp.max(jnp.where(iota(asked.shape, 1) == FLAG, asked, 0))
    spread(asked, scratch)
    for low in range(LOWS):
        table[low * WIDTH : (low + 1) * WIDTH, :] = features_ref[:, low * HIGH : (low + 1) * HIGH]
    one = jnp.bfloat16(1.0)
    zero = jnp.bfloat16(0.0)
    number = iota((PLANE, 2 * LANES), 0).astype(jnp.float32).astype(jnp.bfloat16)
    for peer in range(0, PEERS, 4):
        index = jnp.concatenate([two_peers(scratch, peer + 2 * h) for h in range(2)], axis=1)
        chosen = []
        for k in range(HIGH // PLANE):
            here = (index >> 8) & (HIGH // PLANE - 1)
            key = jnp.where(here == k, index & (PLANE - 1), -1).astype(jnp.float32).astype(jnp.bfloat16)
            chosen.append(jnp.where(number == key, one, zero))
        rows = jnp.dot(
            table[...], jnp.concatenate(chosen, axis=0), preferred_element_type=jnp.float32
        )
        low = index // HIGH
        out = rows[:WIDTH]
        for k in range(1, LOWS):
            out = jnp.where(low == k, rows[k * WIDTH : (k + 1) * WIDTH], out)
        for h in range(2):
            half = out[:, h * LANES : (h + 1) * LANES]
            for x, tile in enumerate(swap(half[:PART], half[PART:])):
                found_ref[peer + 2 * h + x, :, :] = tile.astype(jnp.bfloat16)


def sums_of(reply_ref, code_ref, scratch, targets):
    spread(code_ref[...], scratch)
    row = iota((2 * targets, 2 * LANES), 0)
    wanted = jnp.where(row < targets, -(row + 1), row - targets + 1)
    wanted = wanted.astype(jnp.float32).astype(jnp.bfloat16)
    one = jnp.bfloat16(1.0)
    zero = jnp.bfloat16(0.0)
    members, columns = [], []
    for peer in range(0, PEERS, 4):
        code = jnp.concatenate([two_peers(scratch, peer + 2 * h) for h in range(2)], axis=1)
        members.append(jnp.where(wanted == code.astype(jnp.bfloat16), one, zero))
        for h in range(2):
            tiles = [reply_ref[peer + 2 * h + x].astype(jnp.float32) for x in range(2)]
            rows = [tile.astype(jnp.bfloat16) for tile in [jnp.concatenate(swap(*tiles), axis=0)]]
            columns.append(
                jnp.concatenate(rows + rows + [jnp.ones((32, LANES), jnp.bfloat16)], axis=0)
            )
    return lax.dot_general(
        jnp.concatenate(members, axis=1),
        jnp.concatenate(columns, axis=1),
        NT,
        preferred_element_type=jnp.float32,
    )


def finish(sums, targets):
    own = sums[:targets]
    neigh = sums[targets:]
    mean = neigh / neigh[:, 2 * WIDTH : 2 * WIDTH + 1]
    return jnp.where(iota(own.shape, 1) < WIDTH, own, mean).astype(jnp.bfloat16)


def mean_kernel(reply_ref, code_ref, out_ref, sums_ref, scratch):
    sums = sums_of(reply_ref, code_ref, scratch, out_ref.shape[0])
    sums_ref[...] = sums
    out_ref[...] = finish(sums, out_ref.shape[0])


def rest_kernel(reply_ref, code_ref, sums_ref, out_ref, scratch):
    sums = sums_ref[...] + sums_of(reply_ref, code_ref, scratch, out_ref.shape[0])
    out_ref[...] = finish(sums, out_ref.shape[0])


def layers_kernel(
    part_ref,
    w1_self_ref,
    w1_neigh_ref,
    bias_one_ref,
    w2_self_ref,
    w2_neigh_ref,
    bias_two_ref,
    neighbours_ref,
    count_ref,
    out_ref,
):
    parts = [part_ref[i].astype(jnp.float32) for i in range(part_ref.shape[0])]
    own = jnp.concatenate([p[:, :WIDTH] for p in parts], axis=1).astype(jnp.bfloat16)
    mean = jnp.concatenate([p[:, WIDTH : 2 * WIDTH] for p in parts], axis=1).astype(jnp.bfloat16)
    pre = jnp.dot(own, w1_self_ref[...], preferred_element_type=jnp.float32) + jnp.dot(
        mean, w1_neigh_ref[...], preferred_element_type=jnp.float32
    )
    hidden = jnp.maximum(pre + bias_one_ref[...], 0.0).astype(jnp.bfloat16)
    lane = iota((BLOCK, BLOCK), 1)
    count = jnp.sum(
        jnp.where(lane == iota((BLOCK, BLOCK), 0), count_ref[...].astype(jnp.float32), 0.0),
        axis=1,
        keepdims=True,
    )
    member = jnp.zeros((BLOCK, BLOCK), jnp.float32)
    for j in range(K2):
        named = (neighbours_ref[:, j : j + 1] == lane) & (count > j)
        member = member + jnp.where(named, 1.0, 0.0)
    sums = jnp.dot(member.astype(jnp.bfloat16), hidden, preferred_element_type=jnp.float32)
    mean_two = (sums / count).astype(jnp.bfloat16)
    total = jnp.dot(hidden, w2_self_ref[...], preferred_element_type=jnp.float32) + jnp.dot(
        mean_two, w2_neigh_ref[...], preferred_element_type=jnp.float32
    )
    out_ref[...] = (total + bias_two_ref[...]).astype(jnp.bfloat16)


def call(kernel, out_shape, scratch_shapes, flops, *operands, space=VMEM, out_specs=None):
    return pl.pallas_call(
        kernel,
        out_shape=out_shape,
        in_specs=[pl.BlockSpec(memory_space=space)] * len(operands),
        out_specs=out_specs or jax.tree.map(lambda _: pl.BlockSpec(memory_space=VMEM), out_shape),
        scratch_shapes=scratch_shapes,
        compiler_params=pltpu.CompilerParams(vmem_limit_bytes=LIMIT),
        cost_estimate=pl.CostEstimate(flops=flops, bytes_accessed=1 << 20, transcendentals=0),
    )(*operands)


def route(owner, row_index, count_one):
    lines = owner.shape[0] // LANES
    return call(
        route_kernel,
        [
            jax.ShapeDtypeStruct((PEERS, 1, LANES), jnp.int32),
            jax.ShapeDtypeStruct((PEERS, LANES), jnp.float32),
        ],
        [
            pltpu.VMEM((lines, LANES), jnp.int32),
            pltpu.VMEM((lines, LANES), jnp.int32),
            pltpu.VMEM((count_one.shape[0] // LANES, LANES), jnp.int32),
            pltpu.SemaphoreType.DMA((3,)),
        ],
        1 << 30,
        *[
            pltpu.with_memory_space_constraint(a.reshape(-1, LANES), pltpu.HBM)
            for a in (owner, row_index, count_one)
        ],
        space=pltpu.HBM,
    )


def find(asked, features):
    return call(
        find_kernel,
        [
            jax.ShapeDtypeStruct((PEERS, PART, LANES), jnp.bfloat16),
            jax.ShapeDtypeStruct((1, 1), jnp.int32),
        ],
        [
            pltpu.VMEM((LOWS * WIDTH, HIGH), jnp.bfloat16),
            pltpu.VMEM((PEERS, LANES), jnp.int32),
        ],
        5 << 30,
        asked,
        features.T,
        out_specs=[pl.BlockSpec(memory_space=VMEM), pl.BlockSpec(memory_space=pltpu.SMEM)],
    )


def means(replies, code, targets):
    return call(
        mean_kernel,
        [
            jax.ShapeDtypeStruct((targets, LANES), jnp.bfloat16),
            jax.ShapeDtypeStruct((2 * targets, LANES), jnp.float32),
        ],
        [pltpu.VMEM((PEERS, LANES), jnp.float32)],
        4 << 30,
        replies,
        code,
    )


def with_rest(replies, code, sums, targets):
    return call(
        rest_kernel,
        jax.ShapeDtypeStruct((targets, LANES), jnp.bfloat16),
        [pltpu.VMEM((PEERS, LANES), jnp.float32)],
        4 << 30,
        replies,
        code,
        sums,
    )


def layers(parts, w1_self, w1_neigh, bias_one, w2_self, w2_neigh, bias_two, neighbours, count):
    return call(
        layers_kernel,
        jax.ShapeDtypeStruct((BLOCK, w2_self.shape[1]), jnp.bfloat16),
        [],
        3 << 30,
        parts,
        w1_self,
        w1_neigh,
        bias_one.reshape(1, -1),
        w2_self,
        w2_neigh,
        bias_two.reshape(1, -1),
        neighbours,
        count.reshape(1, -1),
    )


def later_slots(slots):
    lane = lax.broadcasted_iota(jnp.int32, slots.shape, slots.ndim - 1)
    return jnp.where(
        lane < CAPACITY - USUAL, jnp.roll(slots, -USUAL, axis=-1), jnp.zeros_like(slots)
    )


def exchange(array, axis):
    return lax.all_to_all(array, axis, split_axis=0, concat_axis=0, tiled=True)


def per_device(
    features,
    w1_self,
    w1_neigh,
    bias_one,
    w2_self,
    w2_neigh,
    bias_two,
    owner,
    row_index,
    count_one,
    neighbours_two,
    count_two,
):
    targets = count_one.shape[0]
    requests, code = route(owner, row_index, count_one)
    asked = exchange(requests, "rows")
    found, crowded = find(asked, features)
    mine, sums = means(exchange(found, "rows"), code, targets)

    def more(asked, features, code, sums, mine):
        found, _ = find(later_slots(asked), features)
        return with_rest(exchange(found, "rows"), later_slots(code), sums, targets)

    def no_more(asked, features, code, sums, mine):
        return mine

    mine = lax.cond(crowded[0, 0] > 0, more, no_more, asked, features, code, sums, mine)
    parts = exchange(mine.reshape(-1, BLOCK, LANES), "feat")
    return layers(
        parts, w1_self, w1_neigh, bias_one, w2_self, w2_neigh, bias_two, neighbours_two, count_two
    )


def solution(mesh):
    return jax.shard_map(
        per_device,
        mesh=mesh,
        in_specs=(
            P("rows", "feat"),
            P(),
            P(),
            P(),
            P(),
            P(),
            P(),
            P("rows", None),
            P("rows"),
            P("rows"),
            P(("rows", "feat"), None),
            P(("rows", "feat")),
        ),
        out_specs=P(("rows", "feat"), None),
        check_vma=False,
    )
```

```python
import jax
import jax.numpy as jnp
from jax import lax
from jax.experimental import pallas as pl
from jax.experimental.pallas import tpu as pltpu
from jax.sharding import PartitionSpec as P

K1 = 15
K2 = 10
LANES = 128
PEERS = 64
CAPACITY = 80
USUAL = 64
FLAG = LANES - 1
WIDTH = 48
PART = WIDTH // 2
HIGH = 512
PLANE = 256
LOWS = 8
BLOCK = 16
VMEM = pltpu.VMEM
LIMIT = 12 * 1024 * 1024
NT = (((1,), (1,)), ((), ()))


def iota(shape, dimension):
    return lax.broadcasted_iota(jnp.int32, shape, dimension)


def bring(pairs, arrived):
    copies = [pltpu.make_async_copy(a, b, arrived.at[i]) for i, (a, b) in enumerate(pairs)]
    for copy in copies:
        copy.start()
    return copies


def route_kernel(
    owner_hbm,
    row_hbm,
    count_hbm,
    w_self_hbm,
    w_neigh_hbm,
    request_ref,
    code_ref,
    w_self_ref,
    w_neigh_ref,
    owner_ref,
    row_ref,
    count_ref,
    arrived,
    weights_arrived,
):
    copies = bring(
        ((owner_hbm, owner_ref), (row_hbm, row_ref), (count_hbm, count_ref)), arrived
    )
    weights = bring(((w_self_hbm, w_self_ref), (w_neigh_hbm, w_neigh_ref)), weights_arrived)
    for copy in copies:
        copy.wait()
    chunks = owner_ref.shape[0]
    per_chunk = LANES // (K1 + 1)
    half = chunks // 2
    chunk = iota((chunks, LANES), 0)
    lane = iota((chunks, LANES), 1)
    count = count_ref[...].astype(jnp.float32)
    spread = jnp.concatenate(
        [jnp.broadcast_to(count[i : i + 1], (half, LANES)) for i in range(2)], axis=0
    )
    spread = jnp.where(lane // per_chunk == chunk % half, spread, 0.0)
    pick = jnp.where(
        iota((LANES, LANES), 0) % per_chunk == iota((LANES, LANES), 1) // (K1 + 1), 1.0, 0.0
    )
    limit = jnp.dot(
        spread.astype(jnp.bfloat16), pick.astype(jnp.bfloat16), preferred_element_type=jnp.float32
    )
    place = lane % (K1 + 1)
    target = (chunk * per_chunk + lane // (K1 + 1) + 1).astype(jnp.float32)
    code = jnp.where(
        place == 0, -target, jnp.where(place.astype(jnp.float32) <= limit, target, 0.0)
    )
    owner = jnp.where(code == 0.0, -1, owner_ref[...])
    mask = owner[:, None, :] == iota((chunks, PEERS, LANES), 1)
    ones = jnp.where(mask, 1.0, 0.0)
    before = iota((LANES, 2 * LANES), 0)
    upto = iota((LANES, 2 * LANES), 1)
    prefix = jnp.where((before < upto) | (upto >= LANES), 1.0, 0.0).astype(jnp.bfloat16)
    sums = jnp.dot(
        ones.astype(jnp.bfloat16).reshape(chunks * PEERS, LANES),
        prefix,
        preferred_element_type=jnp.float32,
    ).reshape(chunks, PEERS, 2 * LANES)

    row = row_ref[...]
    high = (row >> 6).astype(jnp.float32)
    low = (row & 63).astype(jnp.float32)

    offset = jnp.zeros((PEERS, LANES), jnp.float32)
    total = jnp.zeros((3 * PEERS, CAPACITY), jnp.float32)
    slot = iota((CAPACITY, LANES), 0).astype(jnp.float32)
    values, slots = [], []
    for c in range(chunks):
        here = mask[c]
        rank = jnp.sum(
            jnp.where(here, sums[c, :, :LANES] + offset, 0.0), axis=0, keepdims=True
        )
        offset = offset + sums[c, :, LANES:]
        slots.append(jnp.where(slot == rank, 1.0, 0.0).astype(jnp.bfloat16))
        values.append(
            jnp.concatenate(
                [jnp.where(here, v[c : c + 1], 0.0) for v in (high, low, code)], axis=0
            ).astype(jnp.bfloat16)
        )
        if c % 2 == 1:
            total = total + lax.dot_general(
                jnp.concatenate(values, axis=1),
                jnp.concatenate(slots, axis=1),
                NT,
                preferred_element_type=jnp.float32,
            )
            values, slots = [], []
    crowded = jnp.where(jnp.max(offset) > USUAL, 1, 0)
    request_ref[...] = jnp.where(iota(request_ref.shape, 2) == FLAG, crowded, 0)
    code_ref[...] = jnp.zeros_like(code_ref)
    request_ref[:, 0, :CAPACITY] = (
        total[:PEERS] * 64.0 + total[PEERS : 2 * PEERS]
    ).astype(jnp.int32)
    code_ref[:, :CAPACITY] = total[2 * PEERS :]
    for copy in weights:
        copy.wait()


def spread(slots, scratch):
    lane = iota(slots.shape, 1)
    scratch[...] = jnp.where(lane < USUAL, slots, pltpu.roll(slots, USUAL, 1))


def two_peers(scratch, peer):
    lane = iota((1, LANES), 1)
    return jnp.where(lane < USUAL, scratch[peer : peer + 1, :], scratch[peer + 1 : peer + 2, :])


def swap(first, second):
    lane = iota(first.shape, 1)
    return (
        jnp.where(lane < USUAL, first, pltpu.roll(second, USUAL, 1)),
        jnp.where(lane < USUAL, pltpu.roll(first, USUAL, 1), second),
    )


def find_first_kernel(
    asked_ref,
    features_ref,
    w_self_hbm,
    w_neigh_hbm,
    found_ref,
    crowded_ref,
    w_self_ref,
    w_neigh_ref,
    table,
    scratch,
    weights_arrived,
):
    weights = bring(((w_self_hbm, w_self_ref), (w_neigh_hbm, w_neigh_ref)), weights_arrived)
    asked = asked_ref[:, 0, :]
    crowded_ref[0, 0] = jnp.max(jnp.where(iota(asked.shape, 1) == FLAG, asked, 0))
    find_kernel(asked_ref, features_ref, found_ref, table, scratch)
    for copy in weights:
        copy.wait()


def find_kernel(asked_ref, features_ref, found_ref, table, scratch):
    spread(asked_ref[:, 0, :], scratch)
    for low in range(LOWS):
        table[low * WIDTH : (low + 1) * WIDTH, :] = features_ref[:, low * HIGH : (low + 1) * HIGH]
    one = jnp.bfloat16(1.0)
    zero = jnp.bfloat16(0.0)
    number = iota((PLANE, 2 * LANES), 0).astype(jnp.float32).astype(jnp.bfloat16)
    for peer in range(0, PEERS, 4):
        index = jnp.concatenate([two_peers(scratch, peer + 2 * h) for h in range(2)], axis=1)
        chosen = []
        for k in range(HIGH // PLANE):
            here = (index >> 8) & (HIGH // PLANE - 1)
            key = jnp.where(here == k, index & (PLANE - 1), -1).astype(jnp.float32).astype(jnp.bfloat16)
            chosen.append(jnp.where(number == key, one, zero))
        rows = jnp.dot(
            table[...], jnp.concatenate(chosen, axis=0), preferred_element_type=jnp.float32
        )
        low = index // HIGH
        out = rows[:WIDTH]
        for k in range(1, LOWS):
            out = jnp.where(low == k, rows[k * WIDTH : (k + 1) * WIDTH], out)
        for h in range(2):
            half = out[:, h * LANES : (h + 1) * LANES]
            for x, tile in enumerate(swap(half[:PART], half[PART:])):
                found_ref[peer + 2 * h + x, :, :] = tile.astype(jnp.bfloat16)


def sums_of(reply_ref, code_ref, scratch, targets):
    spread(code_ref[...], scratch)
    row = iota((2 * targets, 2 * LANES), 0)
    wanted = jnp.where(row < targets, -(row + 1), row - targets + 1)
    wanted = wanted.astype(jnp.float32).astype(jnp.bfloat16)
    one = jnp.bfloat16(1.0)
    zero = jnp.bfloat16(0.0)
    members, columns = [], []
    for peer in range(0, PEERS, 4):
        code = jnp.concatenate([two_peers(scratch, peer + 2 * h) for h in range(2)], axis=1)
        members.append(jnp.where(wanted == code.astype(jnp.bfloat16), one, zero))
        for h in range(2):
            tiles = [reply_ref[peer + 2 * h + x].astype(jnp.float32) for x in range(2)]
            rows = [tile.astype(jnp.bfloat16) for tile in [jnp.concatenate(swap(*tiles), axis=0)]]
            columns.append(
                jnp.concatenate(rows + rows + [jnp.ones((32, LANES), jnp.bfloat16)], axis=0)
            )
    return lax.dot_general(
        jnp.concatenate(members, axis=1),
        jnp.concatenate(columns, axis=1),
        NT,
        preferred_element_type=jnp.float32,
    )


def mean_kernel(reply_ref, code_ref, rest_ref, out_ref, scratch):
    targets = out_ref.shape[0]
    sums = sums_of(reply_ref, code_ref, scratch, targets) + rest_ref[...]
    own = sums[:targets]
    neigh = sums[targets:]
    mean = neigh / neigh[:, 2 * WIDTH : 2 * WIDTH + 1]
    out_ref[...] = jnp.where(iota(own.shape, 1) < WIDTH, own, mean).astype(jnp.bfloat16)


def rest_kernel(reply_ref, code_ref, sums_ref, scratch):
    sums_ref[...] = sums_of(reply_ref, code_ref, scratch, sums_ref.shape[0] // 2)


def layers_kernel(
    part_ref,
    w1_self_ref,
    w1_neigh_ref,
    bias_one_ref,
    w2_self_ref,
    w2_neigh_ref,
    bias_two_ref,
    neighbours_ref,
    count_ref,
    out_ref,
):
    parts = [part_ref[i].astype(jnp.float32) for i in range(part_ref.shape[0])]
    own = jnp.concatenate([p[:, :WIDTH] for p in parts], axis=1).astype(jnp.bfloat16)
    mean = jnp.concatenate([p[:, WIDTH : 2 * WIDTH] for p in parts], axis=1).astype(jnp.bfloat16)
    pre = jnp.dot(own, w1_self_ref[...], preferred_element_type=jnp.float32) + jnp.dot(
        mean, w1_neigh_ref[...], preferred_element_type=jnp.float32
    )
    hidden = jnp.maximum(pre + bias_one_ref[...], 0.0).astype(jnp.bfloat16)
    lane = iota((BLOCK, BLOCK), 1)
    count = jnp.sum(
        jnp.where(lane == iota((BLOCK, BLOCK), 0), count_ref[...].astype(jnp.float32), 0.0),
        axis=1,
        keepdims=True,
    )
    member = jnp.zeros((BLOCK, BLOCK), jnp.float32)
    for j in range(K2):
        named = (neighbours_ref[:, j : j + 1] == lane) & (count > j)
        member = member + jnp.where(named, 1.0, 0.0)
    sums = jnp.dot(member.astype(jnp.bfloat16), hidden, preferred_element_type=jnp.float32)
    mean_two = (sums / count).astype(jnp.bfloat16)
    total = jnp.dot(hidden, w2_self_ref[...], preferred_element_type=jnp.float32) + jnp.dot(
        mean_two, w2_neigh_ref[...], preferred_element_type=jnp.float32
    )
    out_ref[...] = (total + bias_two_ref[...]).astype(jnp.bfloat16)


def call(kernel, out_shape, scratch_shapes, flops, *operands, spaces=None, out_spaces=None):
    spaces = spaces or [VMEM] * len(operands)
    out_spaces = out_spaces or [VMEM] * len(out_shape)
    return pl.pallas_call(
        kernel,
        out_shape=out_shape,
        in_specs=[pl.BlockSpec(memory_space=space) for space in spaces],
        out_specs=[pl.BlockSpec(memory_space=space) for space in out_spaces],
        scratch_shapes=scratch_shapes,
        compiler_params=pltpu.CompilerParams(vmem_limit_bytes=LIMIT),
        cost_estimate=pl.CostEstimate(flops=flops, bytes_accessed=1 << 20, transcendentals=0),
    )(*operands)


def in_hbm(*arrays):
    return [pltpu.with_memory_space_constraint(a, pltpu.HBM) for a in arrays]


def in_vmem(*arrays):
    return [pltpu.VMEM(a.shape, a.dtype) for a in arrays]


def route(owner, row_index, count_one, weights):
    lines = owner.shape[0] // LANES
    return call(
        route_kernel,
        [
            jax.ShapeDtypeStruct((PEERS, 1, LANES), jnp.int32),
            jax.ShapeDtypeStruct((PEERS, LANES), jnp.float32),
            *in_vmem(*weights),
        ],
        [
            pltpu.VMEM((lines, LANES), jnp.int32),
            pltpu.VMEM((lines, LANES), jnp.int32),
            pltpu.VMEM((count_one.shape[0] // LANES, LANES), jnp.int32),
            pltpu.SemaphoreType.DMA((3,)),
            pltpu.SemaphoreType.DMA((2,)),
        ],
        1 << 30,
        *in_hbm(*[a.reshape(-1, LANES) for a in (owner, row_index, count_one)], *weights),
        spaces=[pltpu.HBM] * 5,
    )


def find_scratch():
    return [
        pltpu.VMEM((LOWS * WIDTH, HIGH), jnp.bfloat16),
        pltpu.VMEM((PEERS, LANES), jnp.int32),
    ]


def find_first(asked, features, weights):
    return call(
        find_first_kernel,
        [
            pltpu.VMEM((PEERS, PART, LANES), jnp.bfloat16),
            pltpu.SMEM((1, 1), jnp.int32),
            *in_vmem(*weights),
        ],
        [*find_scratch(), pltpu.SemaphoreType.DMA((2,))],
        5 << 30,
        asked,
        features.T,
        *in_hbm(*weights),
        spaces=[VMEM, VMEM, pltpu.HBM, pltpu.HBM],
        out_spaces=[VMEM, pltpu.SMEM, VMEM, VMEM],
    )


def find(asked, features):
    return call(
        find_kernel,
        [jax.ShapeDtypeStruct((PEERS, PART, LANES), jnp.bfloat16)],
        find_scratch(),
        5 << 30,
        asked,
        features.T,
    )[0]


def means(replies, code, rest):
    return call(
        mean_kernel,
        [jax.ShapeDtypeStruct((rest.shape[0] // 2, LANES), jnp.bfloat16)],
        [pltpu.VMEM((PEERS, LANES), jnp.float32)],
        4 << 30,
        replies,
        code,
        rest,
    )[0]


def rest_sums(replies, code, targets):
    return call(
        rest_kernel,
        [jax.ShapeDtypeStruct((2 * targets, LANES), jnp.float32)],
        [pltpu.VMEM((PEERS, LANES), jnp.float32)],
        4 << 30,
        replies,
        code,
    )[0]


def layers(parts, w1_self, w1_neigh, bias_one, w2_self, w2_neigh, bias_two, neighbours, count):
    return call(
        layers_kernel,
        [jax.ShapeDtypeStruct((BLOCK, w2_self.shape[1]), jnp.bfloat16)],
        [],
        3 << 30,
        parts,
        w1_self,
        w1_neigh,
        bias_one.reshape(1, -1),
        w2_self,
        w2_neigh,
        bias_two.reshape(1, -1),
        neighbours,
        count.reshape(1, -1),
    )[0]


def later_slots(slots):
    lane = lax.broadcasted_iota(jnp.int32, slots.shape, slots.ndim - 1)
    return jnp.where(
        lane < CAPACITY - USUAL, jnp.roll(slots, -USUAL, axis=-1), jnp.zeros_like(slots)
    )


def exchange(array, axis):
    return lax.all_to_all(array, axis, split_axis=0, concat_axis=0, tiled=True)


def per_device(
    features,
    w1_self,
    w1_neigh,
    bias_one,
    w2_self,
    w2_neigh,
    bias_two,
    owner,
    row_index,
    count_one,
    neighbours_two,
    count_two,
):
    targets = count_one.shape[0]
    requests, code, w1_self, w1_neigh = route(owner, row_index, count_one, (w1_self, w1_neigh))
    asked = exchange(requests, "rows")
    found, crowded, w2_self, w2_neigh = find_first(asked, features, (w2_self, w2_neigh))

    def more(asked, features, code):
        found = find(later_slots(asked), features)
        return rest_sums(exchange(found, "rows"), later_slots(code), targets)

    def no_more(asked, features, code):
        return jnp.zeros((2 * targets, LANES), jnp.float32)

    rest = lax.cond(crowded[0, 0] > 0, more, no_more, asked, features, code)
    mine = means(exchange(found, "rows"), code, rest)
    parts = exchange(mine.reshape(-1, BLOCK, LANES), "feat")
    return layers(
        parts, w1_self, w1_neigh, bias_one, w2_self, w2_neigh, bias_two, neighbours_two, count_two
    )


def solution(mesh):
    return jax.shard_map(
        per_device,
        mesh=mesh,
        in_specs=(
            P("rows", "feat"),
            P(),
            P(),
            P(),
            P(),
            P(),
            P(),
            P("rows", None),
            P("rows"),
            P("rows"),
            P(("rows", "feat"), None),
            P(("rows", "feat")),
        ),
        out_specs=P(("rows", "feat"), None),
        check_vma=False,
    )
```

```python
import jax
import jax.numpy as jnp
from jax import lax
from jax.experimental import pallas as pl
from jax.experimental.pallas import tpu as pltpu
from jax.sharding import PartitionSpec as P

K1 = 15
K2 = 10
LANES = 128
PEERS = 64
CAPACITY = 80
USUAL = 64
FLAG = LANES - 1
WIDTH = 48
PART = WIDTH // 2
HIGH = 512
PLANE = 256
LOWS = 8
BLOCK = 16
VMEM = pltpu.VMEM
LIMIT = 12 * 1024 * 1024
NT = (((1,), (1,)), ((), ()))


def iota(shape, dimension):
    return lax.broadcasted_iota(jnp.int32, shape, dimension)


def route_kernel(
    owner_hbm, row_hbm, count_hbm, request_ref, code_ref, owner_ref, row_ref, count_ref, arrived
):
    copies = [
        pltpu.make_async_copy(source, target, arrived.at[i])
        for i, (source, target) in enumerate(
            ((owner_hbm, owner_ref), (row_hbm, row_ref), (count_hbm, count_ref))
        )
    ]
    for copy in copies:
        copy.start()
    for copy in copies:
        copy.wait()
    chunks = owner_ref.shape[0]
    per_chunk = LANES // (K1 + 1)
    half = chunks // 2
    chunk = iota((chunks, LANES), 0)
    lane = iota((chunks, LANES), 1)
    count = count_ref[...].astype(jnp.float32)
    spread = jnp.concatenate(
        [jnp.broadcast_to(count[i : i + 1], (half, LANES)) for i in range(2)], axis=0
    )
    spread = jnp.where(lane // per_chunk == chunk % half, spread, 0.0)
    pick = jnp.where(
        iota((LANES, LANES), 0) % per_chunk == iota((LANES, LANES), 1) // (K1 + 1), 1.0, 0.0
    )
    limit = jnp.dot(
        spread.astype(jnp.bfloat16), pick.astype(jnp.bfloat16), preferred_element_type=jnp.float32
    )
    place = lane % (K1 + 1)
    target = (chunk * per_chunk + lane // (K1 + 1) + 1).astype(jnp.float32)
    code = jnp.where(
        place == 0, -target, jnp.where(place.astype(jnp.float32) <= limit, target, 0.0)
    )
    owner = jnp.where(code == 0.0, -1, owner_ref[...])
    mask = owner[:, None, :] == iota((chunks, PEERS, LANES), 1)
    ones = jnp.where(mask, 1.0, 0.0)
    before = iota((LANES, 2 * LANES), 0)
    upto = iota((LANES, 2 * LANES), 1)
    prefix = jnp.where((before < upto) | (upto >= LANES), 1.0, 0.0).astype(jnp.bfloat16)
    sums = jnp.dot(
        ones.astype(jnp.bfloat16).reshape(chunks * PEERS, LANES),
        prefix,
        preferred_element_type=jnp.float32,
    ).reshape(chunks, PEERS, 2 * LANES)

    row = row_ref[...]
    high = (row >> 6).astype(jnp.float32)
    low = (row & 63).astype(jnp.float32)

    offset = jnp.zeros((PEERS, LANES), jnp.float32)
    total = jnp.zeros((3 * PEERS, CAPACITY), jnp.float32)
    slot = iota((CAPACITY, LANES), 0).astype(jnp.float32)
    values, slots = [], []
    for c in range(chunks):
        here = mask[c]
        rank = jnp.sum(
            jnp.where(here, sums[c, :, :LANES] + offset, 0.0), axis=0, keepdims=True
        )
        offset = offset + sums[c, :, LANES:]
        slots.append(jnp.where(slot == rank, 1.0, 0.0).astype(jnp.bfloat16))
        values.append(
            jnp.concatenate(
                [jnp.where(here, v[c : c + 1], 0.0) for v in (high, low, code)], axis=0
            ).astype(jnp.bfloat16)
        )
        if c % 2 == 1:
            total = total + lax.dot_general(
                jnp.concatenate(values, axis=1),
                jnp.concatenate(slots, axis=1),
                NT,
                preferred_element_type=jnp.float32,
            )
            values, slots = [], []
    crowded = jnp.where(jnp.max(offset) > USUAL, 1, 0)
    request_ref[...] = jnp.where(iota(request_ref.shape, 2) == FLAG, crowded, 0)
    code_ref[...] = jnp.zeros_like(code_ref)
    request_ref[:, 0, :CAPACITY] = (
        total[:PEERS] * 64.0 + total[PEERS : 2 * PEERS]
    ).astype(jnp.int32)
    code_ref[:, :CAPACITY] = total[2 * PEERS :]


def spread(slots, scratch):
    lane = iota(slots.shape, 1)
    scratch[...] = jnp.where(lane < USUAL, slots, pltpu.roll(slots, USUAL, 1))


def two_peers(scratch, peer):
    lane = iota((1, LANES), 1)
    return jnp.where(lane < USUAL, scratch[peer : peer + 1, :], scratch[peer + 1 : peer + 2, :])


def swap(first, second):
    lane = iota(first.shape, 1)
    return (
        jnp.where(lane < USUAL, first, pltpu.roll(second, USUAL, 1)),
        jnp.where(lane < USUAL, pltpu.roll(first, USUAL, 1), second),
    )


def find_first_kernel(asked_ref, features_ref, found_ref, crowded_ref, table, scratch):
    asked = asked_ref[:, 0, :]
    crowded_ref[0, 0] = jnp.max(jnp.where(iota(asked.shape, 1) == FLAG, asked, 0))
    find_kernel(asked_ref, features_ref, found_ref, table, scratch)


def find_kernel(asked_ref, features_ref, found_ref, table, scratch):
    spread(asked_ref[:, 0, :], scratch)
    for low in range(LOWS):
        table[low * WIDTH : (low + 1) * WIDTH, :] = features_ref[:, low * HIGH : (low + 1) * HIGH]
    one = jnp.bfloat16(1.0)
    zero = jnp.bfloat16(0.0)
    number = iota((PLANE, 2 * LANES), 0).astype(jnp.float32).astype(jnp.bfloat16)
    for peer in range(0, PEERS, 4):
        index = jnp.concatenate([two_peers(scratch, peer + 2 * h) for h in range(2)], axis=1)
        chosen = []
        for k in range(HIGH // PLANE):
            here = (index >> 8) & (HIGH // PLANE - 1)
            key = jnp.where(here == k, index & (PLANE - 1), -1).astype(jnp.float32).astype(jnp.bfloat16)
            chosen.append(jnp.where(number == key, one, zero))
        rows = jnp.dot(
            table[...], jnp.concatenate(chosen, axis=0), preferred_element_type=jnp.float32
        )
        low = index // HIGH
        out = rows[:WIDTH]
        for k in range(1, LOWS):
            out = jnp.where(low == k, rows[k * WIDTH : (k + 1) * WIDTH], out)
        for h in range(2):
            half = out[:, h * LANES : (h + 1) * LANES]
            for x, tile in enumerate(swap(half[:PART], half[PART:])):
                found_ref[peer + 2 * h + x, :, :] = tile.astype(jnp.bfloat16)


def sums_of(reply_ref, code_ref, scratch, targets):
    spread(code_ref[...], scratch)
    row = iota((2 * targets, 2 * LANES), 0)
    wanted = jnp.where(row < targets, -(row + 1), row - targets + 1)
    wanted = wanted.astype(jnp.float32).astype(jnp.bfloat16)
    one = jnp.bfloat16(1.0)
    zero = jnp.bfloat16(0.0)
    members, columns = [], []
    for peer in range(0, PEERS, 4):
        code = jnp.concatenate([two_peers(scratch, peer + 2 * h) for h in range(2)], axis=1)
        members.append(jnp.where(wanted == code.astype(jnp.bfloat16), one, zero))
        for h in range(2):
            tiles = [reply_ref[peer + 2 * h + x].astype(jnp.float32) for x in range(2)]
            rows = [tile.astype(jnp.bfloat16) for tile in [jnp.concatenate(swap(*tiles), axis=0)]]
            columns.append(
                jnp.concatenate(rows + rows + [jnp.ones((32, LANES), jnp.bfloat16)], axis=0)
            )
    return lax.dot_general(
        jnp.concatenate(members, axis=1),
        jnp.concatenate(columns, axis=1),
        NT,
        preferred_element_type=jnp.float32,
    )


def mean_kernel(reply_ref, code_ref, rest_ref, out_ref, scratch):
    targets = out_ref.shape[0]
    sums = sums_of(reply_ref, code_ref, scratch, targets) + rest_ref[...]
    own = sums[:targets]
    neigh = sums[targets:]
    mean = neigh / neigh[:, 2 * WIDTH : 2 * WIDTH + 1]
    out_ref[...] = jnp.where(iota(own.shape, 1) < WIDTH, own, mean).astype(jnp.bfloat16)


def rest_kernel(reply_ref, code_ref, sums_ref, scratch):
    sums_ref[...] = sums_of(reply_ref, code_ref, scratch, sums_ref.shape[0] // 2)


def layers_kernel(
    part_ref,
    w1_self_ref,
    w1_neigh_ref,
    bias_one_ref,
    w2_self_ref,
    w2_neigh_ref,
    bias_two_ref,
    neighbours_ref,
    count_ref,
    out_ref,
):
    parts = [part_ref[i].astype(jnp.float32) for i in range(part_ref.shape[0])]
    own = jnp.concatenate([p[:, :WIDTH] for p in parts], axis=1).astype(jnp.bfloat16)
    mean = jnp.concatenate([p[:, WIDTH : 2 * WIDTH] for p in parts], axis=1).astype(jnp.bfloat16)
    pre = jnp.dot(own, w1_self_ref[...], preferred_element_type=jnp.float32) + jnp.dot(
        mean, w1_neigh_ref[...], preferred_element_type=jnp.float32
    )
    hidden = jnp.maximum(pre + bias_one_ref[...], 0.0).astype(jnp.bfloat16)
    lane = iota((BLOCK, BLOCK), 1)
    count = jnp.sum(
        jnp.where(lane == iota((BLOCK, BLOCK), 0), count_ref[...].astype(jnp.float32), 0.0),
        axis=1,
        keepdims=True,
    )
    member = jnp.zeros((BLOCK, BLOCK), jnp.float32)
    for j in range(K2):
        named = (neighbours_ref[:, j : j + 1] == lane) & (count > j)
        member = member + jnp.where(named, 1.0, 0.0)
    sums = jnp.dot(member.astype(jnp.bfloat16), hidden, preferred_element_type=jnp.float32)
    mean_two = (sums / count).astype(jnp.bfloat16)
    total = jnp.dot(hidden, w2_self_ref[...], preferred_element_type=jnp.float32) + jnp.dot(
        mean_two, w2_neigh_ref[...], preferred_element_type=jnp.float32
    )
    out_ref[...] = (total + bias_two_ref[...]).astype(jnp.bfloat16)


def call(kernel, out_shape, scratch_shapes, flops, *operands, spaces=None, out_spaces=None):
    spaces = spaces or [VMEM] * len(operands)
    out_spaces = out_spaces or [VMEM] * len(out_shape)
    return pl.pallas_call(
        kernel,
        out_shape=out_shape,
        in_specs=[pl.BlockSpec(memory_space=space) for space in spaces],
        out_specs=[pl.BlockSpec(memory_space=space) for space in out_spaces],
        scratch_shapes=scratch_shapes,
        compiler_params=pltpu.CompilerParams(vmem_limit_bytes=LIMIT),
        cost_estimate=pl.CostEstimate(flops=flops, bytes_accessed=1 << 20, transcendentals=0),
    )(*operands)


def route(owner, row_index, count_one):
    lines = owner.shape[0] // LANES
    return call(
        route_kernel,
        [
            jax.ShapeDtypeStruct((PEERS, 1, LANES), jnp.int32),
            jax.ShapeDtypeStruct((PEERS, LANES), jnp.float32),
        ],
        [
            pltpu.VMEM((lines, LANES), jnp.int32),
            pltpu.VMEM((lines, LANES), jnp.int32),
            pltpu.VMEM((count_one.shape[0] // LANES, LANES), jnp.int32),
            pltpu.SemaphoreType.DMA((3,)),
        ],
        1 << 30,
        *[
            pltpu.with_memory_space_constraint(a.reshape(-1, LANES), pltpu.HBM)
            for a in (owner, row_index, count_one)
        ],
        spaces=[pltpu.HBM] * 3,
    )


def find_scratch():
    return [
        pltpu.VMEM((LOWS * WIDTH, HIGH), jnp.bfloat16),
        pltpu.VMEM((PEERS, LANES), jnp.int32),
    ]


def find_first(asked, features):
    return call(
        find_first_kernel,
        [
            pltpu.VMEM((PEERS, PART, LANES), jnp.bfloat16),
            pltpu.SMEM((1, 1), jnp.int32),
        ],
        find_scratch(),
        5 << 30,
        asked,
        features.T,
        out_spaces=[VMEM, pltpu.SMEM],
    )


def find(asked, features):
    return call(
        find_kernel,
        [jax.ShapeDtypeStruct((PEERS, PART, LANES), jnp.bfloat16)],
        find_scratch(),
        5 << 30,
        asked,
        features.T,
    )[0]


def means(replies, code, rest):
    return call(
        mean_kernel,
        [jax.ShapeDtypeStruct((rest.shape[0] // 2, LANES), jnp.bfloat16)],
        [pltpu.VMEM((PEERS, LANES), jnp.float32)],
        4 << 30,
        replies,
        code,
        rest,
    )[0]


def rest_sums(replies, code, targets):
    return call(
        rest_kernel,
        [jax.ShapeDtypeStruct((2 * targets, LANES), jnp.float32)],
        [pltpu.VMEM((PEERS, LANES), jnp.float32)],
        4 << 30,
        replies,
        code,
    )[0]


def layers(parts, w1_self, w1_neigh, bias_one, w2_self, w2_neigh, bias_two, neighbours, count):
    return call(
        layers_kernel,
        [jax.ShapeDtypeStruct((BLOCK, w2_self.shape[1]), jnp.bfloat16)],
        [],
        3 << 30,
        parts,
        w1_self,
        w1_neigh,
        bias_one.reshape(1, -1),
        w2_self,
        w2_neigh,
        bias_two.reshape(1, -1),
        neighbours,
        count.reshape(1, -1),
    )[0]


def later_slots(slots):
    lane = lax.broadcasted_iota(jnp.int32, slots.shape, slots.ndim - 1)
    return jnp.where(
        lane < CAPACITY - USUAL, jnp.roll(slots, -USUAL, axis=-1), jnp.zeros_like(slots)
    )


def exchange(array, axis):
    return lax.all_to_all(array, axis, split_axis=0, concat_axis=0, tiled=True)


def per_device(
    features,
    w1_self,
    w1_neigh,
    bias_one,
    w2_self,
    w2_neigh,
    bias_two,
    owner,
    row_index,
    count_one,
    neighbours_two,
    count_two,
):
    targets = count_one.shape[0]
    requests, code = route(owner, row_index, count_one)
    asked = exchange(requests, "rows")
    found, crowded = find_first(asked, features)

    def more(asked, features, code):
        found = find(later_slots(asked), features)
        return rest_sums(exchange(found, "rows"), later_slots(code), targets)

    def no_more(asked, features, code):
        return jnp.zeros((2 * targets, LANES), jnp.float32)

    rest = lax.cond(crowded[0, 0] > 0, more, no_more, asked, features, code)
    mine = means(exchange(found, "rows"), code, rest)
    parts = exchange(mine.reshape(-1, BLOCK, LANES), "feat")
    return layers(
        parts, w1_self, w1_neigh, bias_one, w2_self, w2_neigh, bias_two, neighbours_two, count_two
    )


def solution(mesh):
    return jax.shard_map(
        per_device,
        mesh=mesh,
        in_specs=(
            P("rows", "feat"),
            P(),
            P(),
            P(),
            P(),
            P(),
            P(),
            P("rows", None),
            P("rows"),
            P("rows"),
            P(("rows", "feat"), None),
            P(("rows", "feat")),
        ),
        out_specs=P(("rows", "feat"), None),
        check_vma=False,
    )
```

```python
import jax
import jax.numpy as jnp
from jax import lax
from jax.experimental import pallas as pl
from jax.experimental.pallas import tpu as pltpu
from jax.sharding import PartitionSpec as P

K1 = 15
K2 = 10
LANES = 128
PEERS = 64
CAPACITY = 80
USUAL = 64
FLAG = LANES - 1
WIDTH = 48
PART = WIDTH // 2
HIGH = 512
PLANE = 256
LOWS = 8
BLOCK = 16
VMEM = pltpu.VMEM
LIMIT = 12 * 1024 * 1024
NT = (((1,), (1,)), ((), ()))


def iota(shape, dimension):
    return lax.broadcasted_iota(jnp.int32, shape, dimension)


def route_kernel(
    owner_hbm, row_hbm, count_hbm, request_ref, code_ref, owner_ref, row_ref, count_ref, arrived
):
    copies = [
        pltpu.make_async_copy(source, target, arrived.at[i])
        for i, (source, target) in enumerate(
            ((owner_hbm, owner_ref), (row_hbm, row_ref), (count_hbm, count_ref))
        )
    ]
    for copy in copies:
        copy.start()
    for copy in copies:
        copy.wait()
    chunks = owner_ref.shape[0]
    per_chunk = LANES // (K1 + 1)
    half = chunks // 2
    chunk = iota((chunks, LANES), 0)
    lane = iota((chunks, LANES), 1)
    count = count_ref[...].astype(jnp.float32)
    spread = jnp.concatenate(
        [jnp.broadcast_to(count[i : i + 1], (half, LANES)) for i in range(2)], axis=0
    )
    spread = jnp.where(lane // per_chunk == chunk % half, spread, 0.0)
    pick = jnp.where(
        iota((LANES, LANES), 0) % per_chunk == iota((LANES, LANES), 1) // (K1 + 1), 1.0, 0.0
    )
    limit = jnp.dot(
        spread.astype(jnp.bfloat16), pick.astype(jnp.bfloat16), preferred_element_type=jnp.float32
    )
    place = lane % (K1 + 1)
    target = (chunk * per_chunk + lane // (K1 + 1) + 1).astype(jnp.float32)
    code = jnp.where(
        place == 0, -target, jnp.where(place.astype(jnp.float32) <= limit, target, 0.0)
    )
    owner = jnp.where(code == 0.0, -1, owner_ref[...])
    mask = owner[:, None, :] == iota((chunks, PEERS, LANES), 1)
    ones = jnp.where(mask, 1.0, 0.0)
    before = iota((LANES, 2 * LANES), 0)
    upto = iota((LANES, 2 * LANES), 1)
    prefix = jnp.where((before < upto) | (upto >= LANES), 1.0, 0.0).astype(jnp.bfloat16)
    sums = jnp.dot(
        ones.astype(jnp.bfloat16).reshape(chunks * PEERS, LANES),
        prefix,
        preferred_element_type=jnp.float32,
    ).reshape(chunks, PEERS, 2 * LANES)

    row = row_ref[...]
    high = (row >> 6).astype(jnp.float32)
    low = (row & 63).astype(jnp.float32)

    offset = jnp.zeros((PEERS, LANES), jnp.float32)
    total = jnp.zeros((3 * PEERS, CAPACITY), jnp.float32)
    slot = iota((CAPACITY, LANES), 0).astype(jnp.float32)
    values, slots = [], []
    for c in range(chunks):
        here = mask[c]
        rank = jnp.sum(
            jnp.where(here, sums[c, :, :LANES] + offset, 0.0), axis=0, keepdims=True
        )
        offset = offset + sums[c, :, LANES:]
        slots.append(jnp.where(slot == rank, 1.0, 0.0).astype(jnp.bfloat16))
        values.append(
            jnp.concatenate(
                [jnp.where(here, v[c : c + 1], 0.0) for v in (high, low, code)], axis=0
            ).astype(jnp.bfloat16)
        )
        if c % 2 == 1:
            total = total + lax.dot_general(
                jnp.concatenate(values, axis=1),
                jnp.concatenate(slots, axis=1),
                NT,
                preferred_element_type=jnp.float32,
            )
            values, slots = [], []
    crowded = jnp.where(jnp.max(offset) > USUAL, 1, 0)
    request_ref[...] = jnp.where(iota(request_ref.shape, 2) == FLAG, crowded, 0)
    code_ref[...] = jnp.zeros_like(code_ref)
    request_ref[:, 0, :CAPACITY] = (
        total[:PEERS] * 64.0 + total[PEERS : 2 * PEERS]
    ).astype(jnp.int32)
    code_ref[:, :CAPACITY] = total[2 * PEERS :]


def spread(slots, scratch):
    lane = iota(slots.shape, 1)
    scratch[...] = jnp.where(lane < USUAL, slots, pltpu.roll(slots, USUAL, 1))


def two_peers(scratch, peer):
    lane = iota((1, LANES), 1)
    return jnp.where(lane < USUAL, scratch[peer : peer + 1, :], scratch[peer + 1 : peer + 2, :])


def swap(first, second):
    lane = iota(first.shape, 1)
    return (
        jnp.where(lane < USUAL, first, pltpu.roll(second, USUAL, 1)),
        jnp.where(lane < USUAL, pltpu.roll(first, USUAL, 1), second),
    )


def find_first_kernel(asked_ref, features_ref, found_ref, crowded_ref, table, scratch):
    asked = asked_ref[:, 0, :]
    crowded_ref[0, 0] = jnp.max(jnp.where(iota(asked.shape, 1) == FLAG, asked, 0))
    find_kernel(asked_ref, features_ref, found_ref, table, scratch)


def find_kernel(asked_ref, features_ref, found_ref, table, scratch):
    spread(asked_ref[:, 0, :], scratch)
    for low in range(LOWS):
        table[low * WIDTH : (low + 1) * WIDTH, :] = features_ref[:, low * HIGH : (low + 1) * HIGH]
    one = jnp.bfloat16(1.0)
    zero = jnp.bfloat16(0.0)
    number = iota((PLANE, 2 * LANES), 0).astype(jnp.float32).astype(jnp.bfloat16)
    for peer in range(0, PEERS, 4):
        index = jnp.concatenate([two_peers(scratch, peer + 2 * h) for h in range(2)], axis=1)
        chosen = []
        for k in range(HIGH // PLANE):
            here = (index >> 8) & (HIGH // PLANE - 1)
            key = jnp.where(here == k, index & (PLANE - 1), -1).astype(jnp.float32).astype(jnp.bfloat16)
            chosen.append(jnp.where(number == key, one, zero))
        rows = jnp.dot(
            table[...], jnp.concatenate(chosen, axis=0), preferred_element_type=jnp.float32
        )
        low = index // HIGH
        out = rows[:WIDTH]
        for k in range(1, LOWS):
            out = jnp.where(low == k, rows[k * WIDTH : (k + 1) * WIDTH], out)
        for h in range(2):
            half = out[:, h * LANES : (h + 1) * LANES]
            for x, tile in enumerate(swap(half[:PART], half[PART:])):
                found_ref[peer + 2 * h + x, :, :] = tile.astype(jnp.bfloat16)


def sums_of(reply_ref, code_ref, scratch, targets):
    spread(code_ref[...], scratch)
    row = iota((2 * targets, 2 * LANES), 0)
    wanted = jnp.where(row < targets, -(row + 1), row - targets + 1)
    wanted = wanted.astype(jnp.float32).astype(jnp.bfloat16)
    one = jnp.bfloat16(1.0)
    zero = jnp.bfloat16(0.0)
    members, columns = [], []
    for peer in range(0, PEERS, 4):
        code = jnp.concatenate([two_peers(scratch, peer + 2 * h) for h in range(2)], axis=1)
        members.append(jnp.where(wanted == code.astype(jnp.bfloat16), one, zero))
        for h in range(2):
            tiles = [reply_ref[peer + 2 * h + x].astype(jnp.float32) for x in range(2)]
            rows = [tile.astype(jnp.bfloat16) for tile in [jnp.concatenate(swap(*tiles), axis=0)]]
            columns.append(
                jnp.concatenate(rows + rows + [jnp.ones((32, LANES), jnp.bfloat16)], axis=0)
            )
    return lax.dot_general(
        jnp.concatenate(members, axis=1),
        jnp.concatenate(columns, axis=1),
        NT,
        preferred_element_type=jnp.float32,
    )


def mean_kernel(reply_ref, code_ref, rest_ref, out_ref, scratch):
    targets = out_ref.shape[0]
    sums = sums_of(reply_ref, code_ref, scratch, targets) + rest_ref[...]
    own = sums[:targets]
    neigh = sums[targets:]
    mean = neigh / neigh[:, 2 * WIDTH : 2 * WIDTH + 1]
    out_ref[...] = jnp.where(iota(own.shape, 1) < WIDTH, own, mean).astype(jnp.bfloat16)


def rest_kernel(reply_ref, code_ref, sums_ref, scratch):
    sums_ref[...] = sums_of(reply_ref, code_ref, scratch, sums_ref.shape[0] // 2)


def layers_kernel(
    part_ref,
    w1_self_ref,
    w1_neigh_ref,
    bias_one_ref,
    w2_self_ref,
    w2_neigh_ref,
    bias_two_ref,
    neighbours_ref,
    count_ref,
    out_ref,
):
    parts = [part_ref[i].astype(jnp.float32) for i in range(part_ref.shape[0])]
    own = jnp.concatenate([p[:, :WIDTH] for p in parts], axis=1).astype(jnp.bfloat16)
    mean = jnp.concatenate([p[:, WIDTH : 2 * WIDTH] for p in parts], axis=1).astype(jnp.bfloat16)
    pre = jnp.dot(own, w1_self_ref[...], preferred_element_type=jnp.float32) + jnp.dot(
        mean, w1_neigh_ref[...], preferred_element_type=jnp.float32
    )
    hidden = jnp.maximum(pre + bias_one_ref[...], 0.0).astype(jnp.bfloat16)
    lane = iota((BLOCK, BLOCK), 1)
    count = jnp.sum(
        jnp.where(lane == iota((BLOCK, BLOCK), 0), count_ref[...].astype(jnp.float32), 0.0),
        axis=1,
        keepdims=True,
    )
    member = jnp.zeros((BLOCK, BLOCK), jnp.float32)
    for j in range(K2):
        named = (neighbours_ref[:, j : j + 1] == lane) & (count > j)
        member = member + jnp.where(named, 1.0, 0.0)
    sums = jnp.dot(member.astype(jnp.bfloat16), hidden, preferred_element_type=jnp.float32)
    mean_two = (sums / count).astype(jnp.bfloat16)
    total = jnp.dot(hidden, w2_self_ref[...], preferred_element_type=jnp.float32) + jnp.dot(
        mean_two, w2_neigh_ref[...], preferred_element_type=jnp.float32
    )
    out_ref[...] = (total + bias_two_ref[...]).astype(jnp.bfloat16)


def call(kernel, out_shape, scratch_shapes, flops, *operands, spaces=None, out_spaces=None):
    spaces = spaces or [VMEM] * len(operands)
    out_spaces = out_spaces or [VMEM] * len(out_shape)
    return pl.pallas_call(
        kernel,
        out_shape=out_shape,
        in_specs=[pl.BlockSpec(memory_space=space) for space in spaces],
        out_specs=[pl.BlockSpec(memory_space=space) for space in out_spaces],
        scratch_shapes=scratch_shapes,
        compiler_params=pltpu.CompilerParams(vmem_limit_bytes=LIMIT),
        cost_estimate=pl.CostEstimate(flops=flops, bytes_accessed=1 << 20, transcendentals=0),
    )(*operands)


def route(owner, row_index, count_one):
    lines = owner.shape[0] // LANES
    return call(
        route_kernel,
        [
            pltpu.VMEM((PEERS, 1, LANES), jnp.int32),
            jax.ShapeDtypeStruct((PEERS, LANES), jnp.float32),
        ],
        [
            pltpu.VMEM((lines, LANES), jnp.int32),
            pltpu.VMEM((lines, LANES), jnp.int32),
            pltpu.VMEM((count_one.shape[0] // LANES, LANES), jnp.int32),
            pltpu.SemaphoreType.DMA((3,)),
        ],
        1 << 30,
        *[
            pltpu.with_memory_space_constraint(a.reshape(-1, LANES), pltpu.HBM)
            for a in (owner, row_index, count_one)
        ],
        spaces=[pltpu.HBM] * 3,
    )


def find_scratch():
    return [
        pltpu.VMEM((LOWS * WIDTH, HIGH), jnp.bfloat16),
        pltpu.VMEM((PEERS, LANES), jnp.int32),
    ]


def find_first(asked, features):
    return call(
        find_first_kernel,
        [
            pltpu.VMEM((PEERS, PART, LANES), jnp.bfloat16),
            pltpu.SMEM((1, 1), jnp.int32),
        ],
        find_scratch(),
        5 << 30,
        asked,
        features.T,
        out_spaces=[VMEM, pltpu.SMEM],
    )


def find(asked, features):
    return call(
        find_kernel,
        [jax.ShapeDtypeStruct((PEERS, PART, LANES), jnp.bfloat16)],
        find_scratch(),
        5 << 30,
        asked,
        features.T,
    )[0]


def means(replies, code, rest):
    return call(
        mean_kernel,
        [jax.ShapeDtypeStruct((rest.shape[0] // 2, LANES), jnp.bfloat16)],
        [pltpu.VMEM((PEERS, LANES), jnp.float32)],
        4 << 30,
        replies,
        code,
        rest,
    )[0]


def rest_sums(replies, code, targets):
    return call(
        rest_kernel,
        [jax.ShapeDtypeStruct((2 * targets, LANES), jnp.float32)],
        [pltpu.VMEM((PEERS, LANES), jnp.float32)],
        4 << 30,
        replies,
        code,
    )[0]


def layers(parts, w1_self, w1_neigh, bias_one, w2_self, w2_neigh, bias_two, neighbours, count):
    return call(
        layers_kernel,
        [jax.ShapeDtypeStruct((BLOCK, w2_self.shape[1]), jnp.bfloat16)],
        [],
        3 << 30,
        parts,
        w1_self,
        w1_neigh,
        bias_one.reshape(1, -1),
        w2_self,
        w2_neigh,
        bias_two.reshape(1, -1),
        neighbours,
        count.reshape(1, -1),
    )[0]


def later_slots(slots):
    lane = lax.broadcasted_iota(jnp.int32, slots.shape, slots.ndim - 1)
    return jnp.where(
        lane < CAPACITY - USUAL, jnp.roll(slots, -USUAL, axis=-1), jnp.zeros_like(slots)
    )


def exchange(array, axis):
    return lax.all_to_all(array, axis, split_axis=0, concat_axis=0, tiled=True)


def per_device(
    features,
    w1_self,
    w1_neigh,
    bias_one,
    w2_self,
    w2_neigh,
    bias_two,
    owner,
    row_index,
    count_one,
    neighbours_two,
    count_two,
):
    targets = count_one.shape[0]
    requests, code = route(owner, row_index, count_one)
    asked = exchange(requests, "rows")
    found, crowded = find_first(asked, features)

    def more(asked, features, code):
        found = find(later_slots(asked), features)
        return rest_sums(exchange(found, "rows"), later_slots(code), targets)

    def no_more(asked, features, code):
        return jnp.zeros((2 * targets, LANES), jnp.float32)

    rest = lax.cond(crowded[0, 0] > 0, more, no_more, asked, features, code)
    mine = means(exchange(found, "rows"), code, rest)
    parts = exchange(mine.reshape(-1, BLOCK, LANES), "feat")
    return layers(
        parts, w1_self, w1_neigh, bias_one, w2_self, w2_neigh, bias_two, neighbours_two, count_two
    )


def solution(mesh):
    return jax.shard_map(
        per_device,
        mesh=mesh,
        in_specs=(
            P("rows", "feat"),
            P(),
            P(),
            P(),
            P(),
            P(),
            P(),
            P("rows", None),
            P("rows"),
            P("rows"),
            P(("rows", "feat"), None),
            P(("rows", "feat")),
        ),
        out_specs=P(("rows", "feat"), None),
        check_vma=False,
    )
```

```python
import jax
import jax.numpy as jnp
from jax import lax
from jax.experimental import pallas as pl
from jax.experimental.pallas import tpu as pltpu
from jax.sharding import PartitionSpec as P

K1 = 15
K2 = 10
LANES = 128
PEERS = 64
CAPACITY = 80
USUAL = 64
FLAG = LANES - 1
WIDTH = 48
PART = WIDTH // 2
HIGH = 512
PLANE = 256
LOWS = 8
BLOCK = 16
VMEM = pltpu.VMEM
LIMIT = 12 * 1024 * 1024
NT = (((1,), (1,)), ((), ()))


def iota(shape, dimension):
    return lax.broadcasted_iota(jnp.int32, shape, dimension)


def route_kernel(
    owner_hbm, row_hbm, count_hbm, request_ref, code_ref, owner_ref, row_ref, count_ref, arrived
):
    copies = [
        pltpu.make_async_copy(source, target, arrived.at[i])
        for i, (source, target) in enumerate(
            ((owner_hbm, owner_ref), (row_hbm, row_ref), (count_hbm, count_ref))
        )
    ]
    for copy in copies:
        copy.start()
    for copy in copies:
        copy.wait()
    chunks = owner_ref.shape[0]
    per_chunk = LANES // (K1 + 1)
    half = chunks // 2
    chunk = iota((chunks, LANES), 0)
    lane = iota((chunks, LANES), 1)
    count = count_ref[...].astype(jnp.float32)
    spread = jnp.concatenate(
        [jnp.broadcast_to(count[i : i + 1], (half, LANES)) for i in range(2)], axis=0
    )
    spread = jnp.where(lane // per_chunk == chunk % half, spread, 0.0)
    pick = jnp.where(
        iota((LANES, LANES), 0) % per_chunk == iota((LANES, LANES), 1) // (K1 + 1), 1.0, 0.0
    )
    limit = jnp.dot(
        spread.astype(jnp.bfloat16), pick.astype(jnp.bfloat16), preferred_element_type=jnp.float32
    )
    place = lane % (K1 + 1)
    target = (chunk * per_chunk + lane // (K1 + 1) + 1).astype(jnp.float32)
    code = jnp.where(
        place == 0, -target, jnp.where(place.astype(jnp.float32) <= limit, target, 0.0)
    )
    owner = jnp.where(code == 0.0, -1, owner_ref[...])
    mask = owner[:, None, :] == iota((chunks, PEERS, LANES), 1)
    ones = jnp.where(mask, 1.0, 0.0)
    before = iota((LANES, 2 * LANES), 0)
    upto = iota((LANES, 2 * LANES), 1)
    prefix = jnp.where((before < upto) | (upto >= LANES), 1.0, 0.0).astype(jnp.bfloat16)
    sums = jnp.dot(
        ones.astype(jnp.bfloat16).reshape(chunks * PEERS, LANES),
        prefix,
        preferred_element_type=jnp.float32,
    ).reshape(chunks, PEERS, 2 * LANES)

    row = row_ref[...]
    high = (row >> 6).astype(jnp.float32)
    low = (row & 63).astype(jnp.float32)

    offset = jnp.zeros((PEERS, LANES), jnp.float32)
    total = jnp.zeros((3 * PEERS, CAPACITY), jnp.float32)
    slot = iota((CAPACITY, LANES), 0).astype(jnp.float32)
    values, slots = [], []
    for c in range(chunks):
        here = mask[c]
        rank = jnp.sum(
            jnp.where(here, sums[c, :, :LANES] + offset, 0.0), axis=0, keepdims=True
        )
        offset = offset + sums[c, :, LANES:]
        slots.append(jnp.where(slot == rank, 1.0, 0.0).astype(jnp.bfloat16))
        values.append(
            jnp.concatenate(
                [jnp.where(here, v[c : c + 1], 0.0) for v in (high, low, code)], axis=0
            ).astype(jnp.bfloat16)
        )
        if c % 2 == 1:
            total = total + lax.dot_general(
                jnp.concatenate(values, axis=1),
                jnp.concatenate(slots, axis=1),
                NT,
                preferred_element_type=jnp.float32,
            )
            values, slots = [], []
    crowded = jnp.where(jnp.max(offset) > USUAL, 1, 0)
    request_ref[...] = jnp.where(iota(request_ref.shape, 2) == FLAG, crowded, 0)
    code_ref[...] = jnp.zeros_like(code_ref)
    request_ref[:, 0, :CAPACITY] = (
        total[:PEERS] * 64.0 + total[PEERS : 2 * PEERS]
    ).astype(jnp.int32)
    code_ref[:, :CAPACITY] = total[2 * PEERS :]


def spread(slots, scratch):
    lane = iota(slots.shape, 1)
    scratch[...] = jnp.where(lane < USUAL, slots, pltpu.roll(slots, USUAL, 1))


def two_peers(scratch, peer):
    lane = iota((1, LANES), 1)
    return jnp.where(lane < USUAL, scratch[peer : peer + 1, :], scratch[peer + 1 : peer + 2, :])


def swap(first, second):
    lane = iota(first.shape, 1)
    return (
        jnp.where(lane < USUAL, first, pltpu.roll(second, USUAL, 1)),
        jnp.where(lane < USUAL, pltpu.roll(first, USUAL, 1), second),
    )


def find_first_kernel(asked_ref, features_ref, found_ref, crowded_ref, none_ref, table, scratch):
    none_ref[...] = jnp.zeros_like(none_ref)
    asked = asked_ref[:, 0, :]
    crowded_ref[0, 0] = jnp.max(jnp.where(iota(asked.shape, 1) == FLAG, asked, 0))
    find_kernel(asked_ref, features_ref, found_ref, table, scratch)


def find_kernel(asked_ref, features_ref, found_ref, table, scratch):
    spread(asked_ref[:, 0, :], scratch)
    for low in range(LOWS):
        table[low * WIDTH : (low + 1) * WIDTH, :] = features_ref[:, low * HIGH : (low + 1) * HIGH]
    one = jnp.bfloat16(1.0)
    zero = jnp.bfloat16(0.0)
    number = iota((PLANE, 2 * LANES), 0).astype(jnp.float32).astype(jnp.bfloat16)
    for peer in range(0, PEERS, 4):
        index = jnp.concatenate([two_peers(scratch, peer + 2 * h) for h in range(2)], axis=1)
        chosen = []
        for k in range(HIGH // PLANE):
            here = (index >> 8) & (HIGH // PLANE - 1)
            key = jnp.where(here == k, index & (PLANE - 1), -1).astype(jnp.float32).astype(jnp.bfloat16)
            chosen.append(jnp.where(number == key, one, zero))
        rows = jnp.dot(
            table[...], jnp.concatenate(chosen, axis=0), preferred_element_type=jnp.float32
        )
        low = index // HIGH
        out = rows[:WIDTH]
        for k in range(1, LOWS):
            out = jnp.where(low == k, rows[k * WIDTH : (k + 1) * WIDTH], out)
        for h in range(2):
            half = out[:, h * LANES : (h + 1) * LANES]
            for x, tile in enumerate(swap(half[:PART], half[PART:])):
                found_ref[peer + 2 * h + x, :, :] = tile.astype(jnp.bfloat16)


def sums_of(reply_ref, code_ref, scratch, targets):
    spread(code_ref[...], scratch)
    row = iota((2 * targets, 2 * LANES), 0)
    wanted = jnp.where(row < targets, -(row + 1), row - targets + 1)
    wanted = wanted.astype(jnp.float32).astype(jnp.bfloat16)
    one = jnp.bfloat16(1.0)
    zero = jnp.bfloat16(0.0)
    members, columns = [], []
    for peer in range(0, PEERS, 4):
        code = jnp.concatenate([two_peers(scratch, peer + 2 * h) for h in range(2)], axis=1)
        members.append(jnp.where(wanted == code.astype(jnp.bfloat16), one, zero))
        for h in range(2):
            tiles = [reply_ref[peer + 2 * h + x].astype(jnp.float32) for x in range(2)]
            rows = [tile.astype(jnp.bfloat16) for tile in [jnp.concatenate(swap(*tiles), axis=0)]]
            columns.append(
                jnp.concatenate(rows + rows + [jnp.ones((32, LANES), jnp.bfloat16)], axis=0)
            )
    return lax.dot_general(
        jnp.concatenate(members, axis=1),
        jnp.concatenate(columns, axis=1),
        NT,
        preferred_element_type=jnp.float32,
    )


def mean_kernel(reply_ref, code_ref, rest_ref, out_ref, scratch):
    targets = out_ref.shape[0]
    sums = sums_of(reply_ref, code_ref, scratch, targets) + rest_ref[...]
    own = sums[:targets]
    neigh = sums[targets:]
    mean = neigh / neigh[:, 2 * WIDTH : 2 * WIDTH + 1]
    out_ref[...] = jnp.where(iota(own.shape, 1) < WIDTH, own, mean).astype(jnp.bfloat16)


def rest_kernel(reply_ref, code_ref, sums_ref, scratch):
    sums_ref[...] = sums_of(reply_ref, code_ref, scratch, sums_ref.shape[0] // 2)


def layers_kernel(
    part_ref,
    w1_self_ref,
    w1_neigh_ref,
    bias_one_ref,
    w2_self_ref,
    w2_neigh_ref,
    bias_two_ref,
    neighbours_ref,
    count_ref,
    out_ref,
):
    parts = [part_ref[i].astype(jnp.float32) for i in range(part_ref.shape[0])]
    own = jnp.concatenate([p[:, :WIDTH] for p in parts], axis=1).astype(jnp.bfloat16)
    mean = jnp.concatenate([p[:, WIDTH : 2 * WIDTH] for p in parts], axis=1).astype(jnp.bfloat16)
    pre = jnp.dot(own, w1_self_ref[...], preferred_element_type=jnp.float32) + jnp.dot(
        mean, w1_neigh_ref[...], preferred_element_type=jnp.float32
    )
    hidden = jnp.maximum(pre + bias_one_ref[...], 0.0).astype(jnp.bfloat16)
    lane = iota((BLOCK, BLOCK), 1)
    count = jnp.sum(
        jnp.where(lane == iota((BLOCK, BLOCK), 0), count_ref[...].astype(jnp.float32), 0.0),
        axis=1,
        keepdims=True,
    )
    member = jnp.zeros((BLOCK, BLOCK), jnp.float32)
    for j in range(K2):
        named = (neighbours_ref[:, j : j + 1] == lane) & (count > j)
        member = member + jnp.where(named, 1.0, 0.0)
    sums = jnp.dot(member.astype(jnp.bfloat16), hidden, preferred_element_type=jnp.float32)
    mean_two = (sums / count).astype(jnp.bfloat16)
    total = jnp.dot(hidden, w2_self_ref[...], preferred_element_type=jnp.float32) + jnp.dot(
        mean_two, w2_neigh_ref[...], preferred_element_type=jnp.float32
    )
    out_ref[...] = (total + bias_two_ref[...]).astype(jnp.bfloat16)


def call(kernel, out_shape, scratch_shapes, flops, *operands, spaces=None, out_spaces=None):
    spaces = spaces or [VMEM] * len(operands)
    out_spaces = out_spaces or [VMEM] * len(out_shape)
    return pl.pallas_call(
        kernel,
        out_shape=out_shape,
        in_specs=[pl.BlockSpec(memory_space=space) for space in spaces],
        out_specs=[pl.BlockSpec(memory_space=space) for space in out_spaces],
        scratch_shapes=scratch_shapes,
        compiler_params=pltpu.CompilerParams(vmem_limit_bytes=LIMIT),
        cost_estimate=pl.CostEstimate(flops=flops, bytes_accessed=1 << 20, transcendentals=0),
    )(*operands)


def route(owner, row_index, count_one):
    lines = owner.shape[0] // LANES
    return call(
        route_kernel,
        [
            pltpu.VMEM((PEERS, 1, LANES), jnp.int32),
            jax.ShapeDtypeStruct((PEERS, LANES), jnp.float32),
        ],
        [
            pltpu.VMEM((lines, LANES), jnp.int32),
            pltpu.VMEM((lines, LANES), jnp.int32),
            pltpu.VMEM((count_one.shape[0] // LANES, LANES), jnp.int32),
            pltpu.SemaphoreType.DMA((3,)),
        ],
        1 << 30,
        *[
            pltpu.with_memory_space_constraint(a.reshape(-1, LANES), pltpu.HBM)
            for a in (owner, row_index, count_one)
        ],
        spaces=[pltpu.HBM] * 3,
    )


def find_scratch():
    return [
        pltpu.VMEM((LOWS * WIDTH, HIGH), jnp.bfloat16),
        pltpu.VMEM((PEERS, LANES), jnp.int32),
    ]


def find_first(asked, features, targets):
    return call(
        find_first_kernel,
        [
            pltpu.VMEM((PEERS, PART, LANES), jnp.bfloat16),
            pltpu.SMEM((1, 1), jnp.int32),
            jax.ShapeDtypeStruct((2 * targets, LANES), jnp.float32),
        ],
        find_scratch(),
        5 << 30,
        asked,
        features.T,
        out_spaces=[VMEM, pltpu.SMEM, VMEM],
    )


def find(asked, features):
    return call(
        find_kernel,
        [jax.ShapeDtypeStruct((PEERS, PART, LANES), jnp.bfloat16)],
        find_scratch(),
        5 << 30,
        asked,
        features.T,
    )[0]


def means(replies, code, rest):
    return call(
        mean_kernel,
        [jax.ShapeDtypeStruct((rest.shape[0] // 2, LANES), jnp.bfloat16)],
        [pltpu.VMEM((PEERS, LANES), jnp.float32)],
        4 << 30,
        replies,
        code,
        rest,
    )[0]


def rest_sums(replies, code, targets):
    return call(
        rest_kernel,
        [jax.ShapeDtypeStruct((2 * targets, LANES), jnp.float32)],
        [pltpu.VMEM((PEERS, LANES), jnp.float32)],
        4 << 30,
        replies,
        code,
    )[0]


def layers(parts, w1_self, w1_neigh, bias_one, w2_self, w2_neigh, bias_two, neighbours, count):
    return call(
        layers_kernel,
        [jax.ShapeDtypeStruct((BLOCK, w2_self.shape[1]), jnp.bfloat16)],
        [],
        3 << 30,
        parts,
        w1_self,
        w1_neigh,
        bias_one.reshape(1, -1),
        w2_self,
        w2_neigh,
        bias_two.reshape(1, -1),
        neighbours,
        count.reshape(1, -1),
    )[0]


def later_slots(slots):
    lane = lax.broadcasted_iota(jnp.int32, slots.shape, slots.ndim - 1)
    return jnp.where(
        lane < CAPACITY - USUAL, jnp.roll(slots, -USUAL, axis=-1), jnp.zeros_like(slots)
    )


def exchange(array, axis):
    return lax.all_to_all(array, axis, split_axis=0, concat_axis=0, tiled=True)


def per_device(
    features,
    w1_self,
    w1_neigh,
    bias_one,
    w2_self,
    w2_neigh,
    bias_two,
    owner,
    row_index,
    count_one,
    neighbours_two,
    count_two,
):
    targets = count_one.shape[0]
    requests, code = route(owner, row_index, count_one)
    asked = exchange(requests, "rows")
    found, crowded, none = find_first(asked, features, targets)

    def more(asked, features, code, none):
        found = find(later_slots(asked), features)
        return rest_sums(exchange(found, "rows"), later_slots(code), targets)

    def no_more(asked, features, code, none):
        return none

    rest = lax.cond(crowded[0, 0] > 0, more, no_more, asked, features, code, none)
    mine = means(exchange(found, "rows"), code, rest)
    parts = exchange(mine.reshape(-1, BLOCK, LANES), "feat")
    return layers(
        parts, w1_self, w1_neigh, bias_one, w2_self, w2_neigh, bias_two, neighbours_two, count_two
    )


def solution(mesh):
    return jax.shard_map(
        per_device,
        mesh=mesh,
        in_specs=(
            P("rows", "feat"),
            P(),
            P(),
            P(),
            P(),
            P(),
            P(),
            P("rows", None),
            P("rows"),
            P("rows"),
            P(("rows", "feat"), None),
            P(("rows", "feat")),
        ),
        out_specs=P(("rows", "feat"), None),
        check_vma=False,
    )
```

```python
import jax
import jax.numpy as jnp
from jax import lax
from jax.experimental import pallas as pl
from jax.experimental.pallas import tpu as pltpu
from jax.sharding import PartitionSpec as P

K1 = 15
K2 = 10
LANES = 128
PEERS = 64
CAPACITY = 80
USUAL = 64
FLAG = LANES - 1
WIDTH = 48
PART = WIDTH // 2
HIGH = 512
PLANE = 256
LOWS = 8
BLOCK = 16
VMEM = pltpu.VMEM
LIMIT = 12 * 1024 * 1024
NT = (((1,), (1,)), ((), ()))


def iota(shape, dimension):
    return lax.broadcasted_iota(jnp.int32, shape, dimension)


def route_kernel(
    owner_hbm, row_hbm, count_hbm, request_ref, code_ref, owner_ref, row_ref, count_ref, arrived
):
    copies = [
        pltpu.make_async_copy(source, target, arrived.at[i])
        for i, (source, target) in enumerate(
            ((owner_hbm, owner_ref), (row_hbm, row_ref), (count_hbm, count_ref))
        )
    ]
    for copy in copies:
        copy.start()
    for copy in copies:
        copy.wait()
    chunks = owner_ref.shape[0]
    per_chunk = LANES // (K1 + 1)
    half = chunks // 2
    chunk = iota((chunks, LANES), 0)
    lane = iota((chunks, LANES), 1)
    count = count_ref[...].astype(jnp.float32)
    spread = jnp.concatenate(
        [jnp.broadcast_to(count[i : i + 1], (half, LANES)) for i in range(2)], axis=0
    )
    spread = jnp.where(lane // per_chunk == chunk % half, spread, 0.0)
    pick = jnp.where(
        iota((LANES, LANES), 0) % per_chunk == iota((LANES, LANES), 1) // (K1 + 1), 1.0, 0.0
    )
    limit = jnp.dot(
        spread.astype(jnp.bfloat16), pick.astype(jnp.bfloat16), preferred_element_type=jnp.float32
    )
    place = lane % (K1 + 1)
    target = (chunk * per_chunk + lane // (K1 + 1) + 1).astype(jnp.float32)
    code = jnp.where(
        place == 0, -target, jnp.where(place.astype(jnp.float32) <= limit, target, 0.0)
    )
    owner = jnp.where(code == 0.0, -1, owner_ref[...])
    mask = owner[:, None, :] == iota((chunks, PEERS, LANES), 1)
    ones = jnp.where(mask, 1.0, 0.0)
    before = iota((LANES, 2 * LANES), 0)
    upto = iota((LANES, 2 * LANES), 1)
    prefix = jnp.where((before < upto) | (upto >= LANES), 1.0, 0.0).astype(jnp.bfloat16)
    sums = jnp.dot(
        ones.astype(jnp.bfloat16).reshape(chunks * PEERS, LANES),
        prefix,
        preferred_element_type=jnp.float32,
    ).reshape(chunks, PEERS, 2 * LANES)

    row = row_ref[...]
    high = (row >> 6).astype(jnp.float32)
    low = (row & 63).astype(jnp.float32)

    offset = jnp.zeros((PEERS, LANES), jnp.float32)
    total = jnp.zeros((3 * PEERS, CAPACITY), jnp.float32)
    slot = iota((CAPACITY, LANES), 0).astype(jnp.float32)
    values, slots = [], []
    for c in range(chunks):
        here = mask[c]
        rank = jnp.sum(
            jnp.where(here, sums[c, :, :LANES] + offset, 0.0), axis=0, keepdims=True
        )
        offset = offset + sums[c, :, LANES:]
        slots.append(jnp.where(slot == rank, 1.0, 0.0).astype(jnp.bfloat16))
        values.append(
            jnp.concatenate(
                [jnp.where(here, v[c : c + 1], 0.0) for v in (high, low, code)], axis=0
            ).astype(jnp.bfloat16)
        )
        if c % 2 == 1:
            total = total + lax.dot_general(
                jnp.concatenate(values, axis=1),
                jnp.concatenate(slots, axis=1),
                NT,
                preferred_element_type=jnp.float32,
            )
            values, slots = [], []
    crowded = jnp.where(jnp.max(offset) > USUAL, 1, 0)
    request_ref[...] = jnp.where(iota(request_ref.shape, 2) == FLAG, crowded, 0)
    code_ref[...] = jnp.zeros_like(code_ref)
    request_ref[:, 0, :CAPACITY] = (
        total[:PEERS] * 64.0 + total[PEERS : 2 * PEERS]
    ).astype(jnp.int32)
    code_ref[:, :CAPACITY] = total[2 * PEERS :]


def spread(slots, scratch):
    lane = iota(slots.shape, 1)
    scratch[...] = jnp.where(lane < USUAL, slots, pltpu.roll(slots, USUAL, 1))


def two_peers(scratch, peer):
    lane = iota((1, LANES), 1)
    return jnp.where(lane < USUAL, scratch[peer : peer + 1, :], scratch[peer + 1 : peer + 2, :])


def swap(first, second):
    lane = iota(first.shape, 1)
    return (
        jnp.where(lane < USUAL, first, pltpu.roll(second, USUAL, 1)),
        jnp.where(lane < USUAL, pltpu.roll(first, USUAL, 1), second),
    )


def find_first_kernel(asked_ref, features_ref, found_ref, crowded_ref, none_ref, table, scratch):
    none_ref[...] = jnp.zeros_like(none_ref)
    asked = asked_ref[:, 0, :]
    crowded_ref[0, 0] = jnp.max(jnp.where(iota(asked.shape, 1) == FLAG, asked, 0))
    find_kernel(asked_ref, features_ref, found_ref, table, scratch)


def find_kernel(asked_ref, features_ref, found_ref, table, scratch):
    spread(asked_ref[:, 0, :], scratch)
    for low in range(LOWS):
        table[low * WIDTH : (low + 1) * WIDTH, :] = features_ref[:, low * HIGH : (low + 1) * HIGH]
    one = jnp.bfloat16(1.0)
    zero = jnp.bfloat16(0.0)
    number = iota((PLANE, 2 * LANES), 0).astype(jnp.float32).astype(jnp.bfloat16)
    for peer in range(0, PEERS, 4):
        index = jnp.concatenate([two_peers(scratch, peer + 2 * h) for h in range(2)], axis=1)
        chosen = []
        for k in range(HIGH // PLANE):
            here = (index >> 8) & (HIGH // PLANE - 1)
            key = jnp.where(here == k, index & (PLANE - 1), -1).astype(jnp.float32).astype(jnp.bfloat16)
            chosen.append(jnp.where(number == key, one, zero))
        rows = jnp.dot(
            table[...], jnp.concatenate(chosen, axis=0), preferred_element_type=jnp.float32
        )
        low = index // HIGH
        out = rows[:WIDTH]
        for k in range(1, LOWS):
            out = jnp.where(low == k, rows[k * WIDTH : (k + 1) * WIDTH], out)
        for h in range(2):
            half = out[:, h * LANES : (h + 1) * LANES]
            for x, tile in enumerate(swap(half[:PART], half[PART:])):
                found_ref[peer + 2 * h + x, :, :] = tile.astype(jnp.bfloat16)


def sums_of(reply_ref, code_ref, scratch, targets):
    spread(code_ref[...], scratch)
    number = iota((targets, 2 * LANES), 0).astype(jnp.float32).astype(jnp.bfloat16)
    one = jnp.bfloat16(1.0)
    zero = jnp.bfloat16(0.0)
    members, columns = [], []
    for peer in range(0, PEERS, 4):
        code = jnp.concatenate([two_peers(scratch, peer + 2 * h) for h in range(2)], axis=1)
        members.append(jnp.where(number == (jnp.abs(code) - 1.0).astype(jnp.bfloat16), one, zero))
        own = jnp.where(code < 0.0, 1.0, 0.0).astype(jnp.bfloat16)
        neigh = jnp.where(code > 0.0, 1.0, 0.0).astype(jnp.bfloat16)
        for h in range(2):
            tiles = [reply_ref[peer + 2 * h + x].astype(jnp.float32) for x in range(2)]
            rows = jnp.concatenate(swap(*tiles), axis=0).astype(jnp.bfloat16)
            lanes = slice(h * LANES, (h + 1) * LANES)
            columns.append(
                jnp.concatenate(
                    [
                        rows * own[:, lanes],
                        rows * neigh[:, lanes],
                        jnp.broadcast_to(neigh[:, lanes], (LANES - 2 * WIDTH, LANES)),
                    ],
                    axis=0,
                )
            )
    return lax.dot_general(
        jnp.concatenate(members, axis=1),
        jnp.concatenate(columns, axis=1),
        NT,
        preferred_element_type=jnp.float32,
    )


def mean_kernel(reply_ref, code_ref, rest_ref, out_ref, scratch):
    sums = sums_of(reply_ref, code_ref, scratch, out_ref.shape[0]) + rest_ref[...]
    mean = sums / sums[:, 2 * WIDTH : 2 * WIDTH + 1]
    out_ref[...] = jnp.where(iota(sums.shape, 1) < WIDTH, sums, mean).astype(jnp.bfloat16)


def rest_kernel(reply_ref, code_ref, sums_ref, scratch):
    sums_ref[...] = sums_of(reply_ref, code_ref, scratch, sums_ref.shape[0])


def layers_kernel(
    part_ref,
    w1_self_ref,
    w1_neigh_ref,
    bias_one_ref,
    w2_self_ref,
    w2_neigh_ref,
    bias_two_ref,
    neighbours_ref,
    count_ref,
    out_ref,
):
    parts = [part_ref[i].astype(jnp.float32) for i in range(part_ref.shape[0])]
    own = jnp.concatenate([p[:, :WIDTH] for p in parts], axis=1).astype(jnp.bfloat16)
    mean = jnp.concatenate([p[:, WIDTH : 2 * WIDTH] for p in parts], axis=1).astype(jnp.bfloat16)
    pre = jnp.dot(own, w1_self_ref[...], preferred_element_type=jnp.float32) + jnp.dot(
        mean, w1_neigh_ref[...], preferred_element_type=jnp.float32
    )
    hidden = jnp.maximum(pre + bias_one_ref[...], 0.0).astype(jnp.bfloat16)
    lane = iota((BLOCK, BLOCK), 1)
    count = jnp.sum(
        jnp.where(lane == iota((BLOCK, BLOCK), 0), count_ref[...].astype(jnp.float32), 0.0),
        axis=1,
        keepdims=True,
    )
    member = jnp.zeros((BLOCK, BLOCK), jnp.float32)
    for j in range(K2):
        named = (neighbours_ref[:, j : j + 1] == lane) & (count > j)
        member = member + jnp.where(named, 1.0, 0.0)
    sums = jnp.dot(member.astype(jnp.bfloat16), hidden, preferred_element_type=jnp.float32)
    mean_two = (sums / count).astype(jnp.bfloat16)
    total = jnp.dot(hidden, w2_self_ref[...], preferred_element_type=jnp.float32) + jnp.dot(
        mean_two, w2_neigh_ref[...], preferred_element_type=jnp.float32
    )
    out_ref[...] = (total + bias_two_ref[...]).astype(jnp.bfloat16)


def call(kernel, out_shape, scratch_shapes, flops, *operands, spaces=None, out_spaces=None):
    spaces = spaces or [VMEM] * len(operands)
    out_spaces = out_spaces or [VMEM] * len(out_shape)
    return pl.pallas_call(
        kernel,
        out_shape=out_shape,
        in_specs=[pl.BlockSpec(memory_space=space) for space in spaces],
        out_specs=[pl.BlockSpec(memory_space=space) for space in out_spaces],
        scratch_shapes=scratch_shapes,
        compiler_params=pltpu.CompilerParams(vmem_limit_bytes=LIMIT),
        cost_estimate=pl.CostEstimate(flops=flops, bytes_accessed=1 << 20, transcendentals=0),
    )(*operands)


def route(owner, row_index, count_one):
    lines = owner.shape[0] // LANES
    return call(
        route_kernel,
        [
            pltpu.VMEM((PEERS, 1, LANES), jnp.int32),
            jax.ShapeDtypeStruct((PEERS, LANES), jnp.float32),
        ],
        [
            pltpu.VMEM((lines, LANES), jnp.int32),
            pltpu.VMEM((lines, LANES), jnp.int32),
            pltpu.VMEM((count_one.shape[0] // LANES, LANES), jnp.int32),
            pltpu.SemaphoreType.DMA((3,)),
        ],
        1 << 30,
        *[
            pltpu.with_memory_space_constraint(a.reshape(-1, LANES), pltpu.HBM)
            for a in (owner, row_index, count_one)
        ],
        spaces=[pltpu.HBM] * 3,
    )


def find_scratch():
    return [
        pltpu.VMEM((LOWS * WIDTH, HIGH), jnp.bfloat16),
        pltpu.VMEM((PEERS, LANES), jnp.int32),
    ]


def find_first(asked, features, targets):
    return call(
        find_first_kernel,
        [
            pltpu.VMEM((PEERS, PART, LANES), jnp.bfloat16),
            pltpu.SMEM((1, 1), jnp.int32),
            jax.ShapeDtypeStruct((targets, LANES), jnp.float32),
        ],
        find_scratch(),
        5 << 30,
        asked,
        features.T,
        out_spaces=[VMEM, pltpu.SMEM, VMEM],
    )


def find(asked, features):
    return call(
        find_kernel,
        [jax.ShapeDtypeStruct((PEERS, PART, LANES), jnp.bfloat16)],
        find_scratch(),
        5 << 30,
        asked,
        features.T,
    )[0]


def means(replies, code, rest):
    return call(
        mean_kernel,
        [jax.ShapeDtypeStruct(rest.shape, jnp.bfloat16)],
        [pltpu.VMEM((PEERS, LANES), jnp.float32)],
        4 << 30,
        replies,
        code,
        rest,
    )[0]


def rest_sums(replies, code, targets):
    return call(
        rest_kernel,
        [jax.ShapeDtypeStruct((targets, LANES), jnp.float32)],
        [pltpu.VMEM((PEERS, LANES), jnp.float32)],
        4 << 30,
        replies,
        code,
    )[0]


def layers(parts, w1_self, w1_neigh, bias_one, w2_self, w2_neigh, bias_two, neighbours, count):
    return call(
        layers_kernel,
        [jax.ShapeDtypeStruct((BLOCK, w2_self.shape[1]), jnp.bfloat16)],
        [],
        3 << 30,
        parts,
        w1_self,
        w1_neigh,
        bias_one.reshape(1, -1),
        w2_self,
        w2_neigh,
        bias_two.reshape(1, -1),
        neighbours,
        count.reshape(1, -1),
    )[0]


def later_slots(slots):
    lane = lax.broadcasted_iota(jnp.int32, slots.shape, slots.ndim - 1)
    return jnp.where(
        lane < CAPACITY - USUAL, jnp.roll(slots, -USUAL, axis=-1), jnp.zeros_like(slots)
    )


def exchange(array, axis):
    return lax.all_to_all(array, axis, split_axis=0, concat_axis=0, tiled=True)


def per_device(
    features,
    w1_self,
    w1_neigh,
    bias_one,
    w2_self,
    w2_neigh,
    bias_two,
    owner,
    row_index,
    count_one,
    neighbours_two,
    count_two,
):
    targets = count_one.shape[0]
    requests, code = route(owner, row_index, count_one)
    asked = exchange(requests, "rows")
    found, crowded, none = find_first(asked, features, targets)

    def more(asked, features, code, none):
        found = find(later_slots(asked), features)
        return rest_sums(exchange(found, "rows"), later_slots(code), targets)

    def no_more(asked, features, code, none):
        return none

    rest = lax.cond(crowded[0, 0] > 0, more, no_more, asked, features, code, none)
    mine = means(exchange(found, "rows"), code, rest)
    parts = exchange(mine.reshape(-1, BLOCK, LANES), "feat")
    return layers(
        parts, w1_self, w1_neigh, bias_one, w2_self, w2_neigh, bias_two, neighbours_two, count_two
    )


def solution(mesh):
    return jax.shard_map(
        per_device,
        mesh=mesh,
        in_specs=(
            P("rows", "feat"),
            P(),
            P(),
            P(),
            P(),
            P(),
            P(),
            P("rows", None),
            P("rows"),
            P("rows"),
            P(("rows", "feat"), None),
            P(("rows", "feat")),
        ),
        out_specs=P(("rows", "feat"), None),
        check_vma=False,
    )
```

```python
import jax
import jax.numpy as jnp
from jax import lax
from jax.experimental import pallas as pl
from jax.experimental.pallas import tpu as pltpu
from jax.sharding import PartitionSpec as P

K1 = 15
K2 = 10
LANES = 128
PEERS = 64
CAPACITY = 80
USUAL = 64
FLAG = LANES - 1
WIDTH = 48
PART = WIDTH // 2
HIGH = 512
PLANE = 256
LOWS = 8
BLOCK = 16
VMEM = pltpu.VMEM
LIMIT = 12 * 1024 * 1024
NT = (((1,), (1,)), ((), ()))


def iota(shape, dimension):
    return lax.broadcasted_iota(jnp.int32, shape, dimension)


def route_kernel(
    owner_hbm, row_hbm, count_hbm, request_ref, code_ref, owner_ref, row_ref, count_ref, arrived
):
    copies = [
        pltpu.make_async_copy(source, target, arrived.at[i])
        for i, (source, target) in enumerate(
            ((owner_hbm, owner_ref), (row_hbm, row_ref), (count_hbm, count_ref))
        )
    ]
    for copy in reversed(copies):
        copy.start()
    chunks = owner_ref.shape[0]
    per_chunk = LANES // (K1 + 1)
    half = chunks // 2
    chunk = iota((chunks, LANES), 0)
    lane = iota((chunks, LANES), 1)
    place = lane % (K1 + 1)
    target = (chunk * per_chunk + lane // (K1 + 1) + 1).astype(jnp.float32)
    pick = jnp.where(
        iota((LANES, LANES), 0) % per_chunk == iota((LANES, LANES), 1) // (K1 + 1), 1.0, 0.0
    ).astype(jnp.bfloat16)
    before = iota((LANES, 2 * LANES), 0)
    upto = iota((LANES, 2 * LANES), 1)
    prefix = jnp.where((before < upto) | (upto >= LANES), 1.0, 0.0).astype(jnp.bfloat16)
    code_ref[...] = jnp.zeros_like(code_ref)
    copies[2].wait()

    count = count_ref[...].astype(jnp.float32)
    spread = jnp.concatenate(
        [jnp.broadcast_to(count[i : i + 1], (half, LANES)) for i in range(2)], axis=0
    )
    spread = jnp.where(lane // per_chunk == chunk % half, spread, 0.0)
    limit = jnp.dot(spread.astype(jnp.bfloat16), pick, preferred_element_type=jnp.float32)
    code = jnp.where(
        place == 0, -target, jnp.where(place.astype(jnp.float32) <= limit, target, 0.0)
    )
    copies[0].wait()
    copies[1].wait()
    owner = jnp.where(code == 0.0, -1, owner_ref[...])
    mask = owner[:, None, :] == iota((chunks, PEERS, LANES), 1)
    ones = jnp.where(mask, 1.0, 0.0)
    sums = jnp.dot(
        ones.astype(jnp.bfloat16).reshape(chunks * PEERS, LANES),
        prefix,
        preferred_element_type=jnp.float32,
    ).reshape(chunks, PEERS, 2 * LANES)

    row = row_ref[...]
    high = (row >> 6).astype(jnp.float32)
    low = (row & 63).astype(jnp.float32)

    offset = jnp.zeros((PEERS, LANES), jnp.float32)
    total = jnp.zeros((3 * PEERS, CAPACITY), jnp.float32)
    slot = iota((CAPACITY, LANES), 0).astype(jnp.float32)
    values, slots = [], []
    for c in range(chunks):
        here = mask[c]
        rank = jnp.sum(
            jnp.where(here, sums[c, :, :LANES] + offset, 0.0), axis=0, keepdims=True
        )
        offset = offset + sums[c, :, LANES:]
        slots.append(jnp.where(slot == rank, 1.0, 0.0).astype(jnp.bfloat16))
        values.append(
            jnp.concatenate(
                [jnp.where(here, v[c : c + 1], 0.0) for v in (high, low, code)], axis=0
            ).astype(jnp.bfloat16)
        )
        if c % 2 == 1:
            total = total + lax.dot_general(
                jnp.concatenate(values, axis=1),
                jnp.concatenate(slots, axis=1),
                NT,
                preferred_element_type=jnp.float32,
            )
            values, slots = [], []
    crowded = jnp.where(jnp.max(offset) > USUAL, 1, 0)
    request_ref[...] = jnp.where(iota(request_ref.shape, 2) == FLAG, crowded, 0)
    request_ref[:, 0, :CAPACITY] = (
        total[:PEERS] * 64.0 + total[PEERS : 2 * PEERS]
    ).astype(jnp.int32)
    code_ref[:, :CAPACITY] = total[2 * PEERS :]


def spread(slots, scratch):
    lane = iota(slots.shape, 1)
    scratch[...] = jnp.where(lane < USUAL, slots, pltpu.roll(slots, USUAL, 1))


def two_peers(scratch, peer):
    lane = iota((1, LANES), 1)
    return jnp.where(lane < USUAL, scratch[peer : peer + 1, :], scratch[peer + 1 : peer + 2, :])


def swap(first, second):
    lane = iota(first.shape, 1)
    return (
        jnp.where(lane < USUAL, first, pltpu.roll(second, USUAL, 1)),
        jnp.where(lane < USUAL, pltpu.roll(first, USUAL, 1), second),
    )


def find_first_kernel(asked_ref, features_ref, found_ref, crowded_ref, none_ref, table, scratch):
    none_ref[...] = jnp.zeros_like(none_ref)
    asked = asked_ref[:, 0, :]
    crowded_ref[0, 0] = jnp.max(jnp.where(iota(asked.shape, 1) == FLAG, asked, 0))
    find_kernel(asked_ref, features_ref, found_ref, table, scratch)


def find_kernel(asked_ref, features_ref, found_ref, table, scratch):
    spread(asked_ref[:, 0, :], scratch)
    for low in range(LOWS):
        table[low * WIDTH : (low + 1) * WIDTH, :] = features_ref[:, low * HIGH : (low + 1) * HIGH]
    one = jnp.bfloat16(1.0)
    zero = jnp.bfloat16(0.0)
    number = iota((PLANE, 2 * LANES), 0).astype(jnp.float32).astype(jnp.bfloat16)
    for peer in range(0, PEERS, 4):
        index = jnp.concatenate([two_peers(scratch, peer + 2 * h) for h in range(2)], axis=1)
        chosen = []
        for k in range(HIGH // PLANE):
            here = (index >> 8) & (HIGH // PLANE - 1)
            key = jnp.where(here == k, index & (PLANE - 1), -1).astype(jnp.float32).astype(jnp.bfloat16)
            chosen.append(jnp.where(number == key, one, zero))
        rows = jnp.dot(
            table[...], jnp.concatenate(chosen, axis=0), preferred_element_type=jnp.float32
        )
        low = index // HIGH
        out = rows[:WIDTH]
        for k in range(1, LOWS):
            out = jnp.where(low == k, rows[k * WIDTH : (k + 1) * WIDTH], out)
        for h in range(2):
            half = out[:, h * LANES : (h + 1) * LANES]
            for x, tile in enumerate(swap(half[:PART], half[PART:])):
                found_ref[peer + 2 * h + x, :, :] = tile.astype(jnp.bfloat16)


def sums_of(reply_ref, code_ref, scratch, targets):
    spread(code_ref[...], scratch)
    number = iota((targets, 2 * LANES), 0).astype(jnp.float32).astype(jnp.bfloat16)
    one = jnp.bfloat16(1.0)
    zero = jnp.bfloat16(0.0)
    members, columns = [], []
    for peer in range(0, PEERS, 4):
        code = jnp.concatenate([two_peers(scratch, peer + 2 * h) for h in range(2)], axis=1)
        members.append(jnp.where(number == (jnp.abs(code) - 1.0).astype(jnp.bfloat16), one, zero))
        own = jnp.where(code < 0.0, 1.0, 0.0).astype(jnp.bfloat16)
        neigh = jnp.where(code > 0.0, 1.0, 0.0).astype(jnp.bfloat16)
        for h in range(2):
            tiles = [reply_ref[peer + 2 * h + x].astype(jnp.float32) for x in range(2)]
            rows = jnp.concatenate(swap(*tiles), axis=0).astype(jnp.bfloat16)
            lanes = slice(h * LANES, (h + 1) * LANES)
            columns.append(
                jnp.concatenate(
                    [
                        rows * own[:, lanes],
                        rows * neigh[:, lanes],
                        jnp.broadcast_to(neigh[:, lanes], (LANES - 2 * WIDTH, LANES)),
                    ],
                    axis=0,
                )
            )
    return lax.dot_general(
        jnp.concatenate(members, axis=1),
        jnp.concatenate(columns, axis=1),
        NT,
        preferred_element_type=jnp.float32,
    )


def mean_kernel(reply_ref, code_ref, rest_ref, out_ref, scratch):
    sums = sums_of(reply_ref, code_ref, scratch, out_ref.shape[0]) + rest_ref[...]
    mean = sums / sums[:, 2 * WIDTH : 2 * WIDTH + 1]
    out_ref[...] = jnp.where(iota(sums.shape, 1) < WIDTH, sums, mean).astype(jnp.bfloat16)


def rest_kernel(reply_ref, code_ref, sums_ref, scratch):
    sums_ref[...] = sums_of(reply_ref, code_ref, scratch, sums_ref.shape[0])


def layers_kernel(
    part_ref,
    w1_self_ref,
    w1_neigh_ref,
    bias_one_ref,
    w2_self_ref,
    w2_neigh_ref,
    bias_two_ref,
    neighbours_ref,
    count_ref,
    out_ref,
):
    parts = [part_ref[i].astype(jnp.float32) for i in range(part_ref.shape[0])]
    own = jnp.concatenate([p[:, :WIDTH] for p in parts], axis=1).astype(jnp.bfloat16)
    mean = jnp.concatenate([p[:, WIDTH : 2 * WIDTH] for p in parts], axis=1).astype(jnp.bfloat16)
    pre = jnp.dot(own, w1_self_ref[...], preferred_element_type=jnp.float32) + jnp.dot(
        mean, w1_neigh_ref[...], preferred_element_type=jnp.float32
    )
    hidden = jnp.maximum(pre + bias_one_ref[...], 0.0).astype(jnp.bfloat16)
    lane = iota((BLOCK, BLOCK), 1)
    count = jnp.sum(
        jnp.where(lane == iota((BLOCK, BLOCK), 0), count_ref[...].astype(jnp.float32), 0.0),
        axis=1,
        keepdims=True,
    )
    member = jnp.zeros((BLOCK, BLOCK), jnp.float32)
    for j in range(K2):
        named = (neighbours_ref[:, j : j + 1] == lane) & (count > j)
        member = member + jnp.where(named, 1.0, 0.0)
    sums = jnp.dot(member.astype(jnp.bfloat16), hidden, preferred_element_type=jnp.float32)
    mean_two = (sums / count).astype(jnp.bfloat16)
    total = jnp.dot(hidden, w2_self_ref[...], preferred_element_type=jnp.float32) + jnp.dot(
        mean_two, w2_neigh_ref[...], preferred_element_type=jnp.float32
    )
    out_ref[...] = (total + bias_two_ref[...]).astype(jnp.bfloat16)


def call(kernel, out_shape, scratch_shapes, flops, *operands, spaces=None, out_spaces=None):
    spaces = spaces or [VMEM] * len(operands)
    out_spaces = out_spaces or [VMEM] * len(out_shape)
    return pl.pallas_call(
        kernel,
        out_shape=out_shape,
        in_specs=[pl.BlockSpec(memory_space=space) for space in spaces],
        out_specs=[pl.BlockSpec(memory_space=space) for space in out_spaces],
        scratch_shapes=scratch_shapes,
        compiler_params=pltpu.CompilerParams(vmem_limit_bytes=LIMIT),
        cost_estimate=pl.CostEstimate(flops=flops, bytes_accessed=1 << 20, transcendentals=0),
    )(*operands)


def route(owner, row_index, count_one):
    lines = owner.shape[0] // LANES
    return call(
        route_kernel,
        [
            pltpu.VMEM((PEERS, 1, LANES), jnp.int32),
            jax.ShapeDtypeStruct((PEERS, LANES), jnp.float32),
        ],
        [
            pltpu.VMEM((lines, LANES), jnp.int32),
            pltpu.VMEM((lines, LANES), jnp.int32),
            pltpu.VMEM((count_one.shape[0] // LANES, LANES), jnp.int32),
            pltpu.SemaphoreType.DMA((3,)),
        ],
        1 << 30,
        *[
            pltpu.with_memory_space_constraint(a.reshape(-1, LANES), pltpu.HBM)
            for a in (owner, row_index, count_one)
        ],
        spaces=[pltpu.HBM] * 3,
    )


def find_scratch():
    return [
        pltpu.VMEM((LOWS * WIDTH, HIGH), jnp.bfloat16),
        pltpu.VMEM((PEERS, LANES), jnp.int32),
    ]


def find_first(asked, features, targets):
    return call(
        find_first_kernel,
        [
            pltpu.VMEM((PEERS, PART, LANES), jnp.bfloat16),
            pltpu.SMEM((1, 1), jnp.int32),
            jax.ShapeDtypeStruct((targets, LANES), jnp.float32),
        ],
        find_scratch(),
        5 << 30,
        asked,
        features.T,
        out_spaces=[VMEM, pltpu.SMEM, VMEM],
    )


def find(asked, features):
    return call(
        find_kernel,
        [jax.ShapeDtypeStruct((PEERS, PART, LANES), jnp.bfloat16)],
        find_scratch(),
        5 << 30,
        asked,
        features.T,
    )[0]


def means(replies, code, rest):
    return call(
        mean_kernel,
        [jax.ShapeDtypeStruct(rest.shape, jnp.bfloat16)],
        [pltpu.VMEM((PEERS, LANES), jnp.float32)],
        4 << 30,
        replies,
        code,
        rest,
    )[0]


def rest_sums(replies, code, targets):
    return call(
        rest_kernel,
        [jax.ShapeDtypeStruct((targets, LANES), jnp.float32)],
        [pltpu.VMEM((PEERS, LANES), jnp.float32)],
        4 << 30,
        replies,
        code,
    )[0]


def layers(parts, w1_self, w1_neigh, bias_one, w2_self, w2_neigh, bias_two, neighbours, count):
    return call(
        layers_kernel,
        [jax.ShapeDtypeStruct((BLOCK, w2_self.shape[1]), jnp.bfloat16)],
        [],
        3 << 30,
        parts,
        w1_self,
        w1_neigh,
        bias_one.reshape(1, -1),
        w2_self,
        w2_neigh,
        bias_two.reshape(1, -1),
        neighbours,
        count.reshape(1, -1),
    )[0]


def later_slots(slots):
    lane = lax.broadcasted_iota(jnp.int32, slots.shape, slots.ndim - 1)
    return jnp.where(
        lane < CAPACITY - USUAL, jnp.roll(slots, -USUAL, axis=-1), jnp.zeros_like(slots)
    )


def exchange(array, axis):
    return lax.all_to_all(array, axis, split_axis=0, concat_axis=0, tiled=True)


def per_device(
    features,
    w1_self,
    w1_neigh,
    bias_one,
    w2_self,
    w2_neigh,
    bias_two,
    owner,
    row_index,
    count_one,
    neighbours_two,
    count_two,
):
    targets = count_one.shape[0]
    requests, code = route(owner, row_index, count_one)
    asked = exchange(requests, "rows")
    found, crowded, none = find_first(asked, features, targets)

    def more(asked, features, code, none):
        found = find(later_slots(asked), features)
        return rest_sums(exchange(found, "rows"), later_slots(code), targets)

    def no_more(asked, features, code, none):
        return none

    rest = lax.cond(crowded[0, 0] > 0, more, no_more, asked, features, code, none)
    mine = means(exchange(found, "rows"), code, rest)
    parts = exchange(mine.reshape(-1, BLOCK, LANES), "feat")
    return layers(
        parts, w1_self, w1_neigh, bias_one, w2_self, w2_neigh, bias_two, neighbours_two, count_two
    )


def solution(mesh):
    return jax.shard_map(
        per_device,
        mesh=mesh,
        in_specs=(
            P("rows", "feat"),
            P(),
            P(),
            P(),
            P(),
            P(),
            P(),
            P("rows", None),
            P("rows"),
            P("rows"),
            P(("rows", "feat"), None),
            P(("rows", "feat")),
        ),
        out_specs=P(("rows", "feat"), None),
        check_vma=False,
    )
```
